128 devices in a mesh: pipe: 8 (over z, core), dp: 8 (over x_lo, y), tensor: 2 (over x_hi).
Axes of the slice: x: 4 (x_hi: 2, x_lo: 2; x = x_hi * 2 + x_lo), y: 4, z: 4, core: 2. Of those that a mesh axis runs over, the one named last changes fastest.
Arguments:
- tokens: bfloat16 [4, 64, 4096], replicated, may hold values from -6 to 6
- slice_order: int32 [4], replicated, may hold values from 0 to 3, each once
- norm_gain: float32 [8, 4096], P('pipe'), may hold values from 0.5 to 1.5
- w_z: bfloat16 [8, 4096, 8192], P('pipe', None, ('dp', 'tensor')), may hold values from -0.09375 to 0.09375
- w_x: bfloat16 [8, 4096, 8192], P('pipe', None, ('dp', 'tensor')), may hold values from -0.09375 to 0.09375
- w_bc: bfloat16 [8, 4096, 2048], P('pipe', None, 'dp'), may hold values from -0.09375 to 0.09375
- w_dt: bfloat16 [8, 4096, 128], P('pipe', None, ('dp', 'tensor')), may hold values from -0.09375 to 0.09375
- conv_x: float32 [8, 4, 8192], P('pipe', None, ('dp', 'tensor')), may hold values from -3 to 3
- conv_bc: float32 [8, 4, 2048], P('pipe', None, 'dp'), may hold values from -3 to 3
- dt_bias: float32 [8, 128], P('pipe', ('dp', 'tensor')), may hold values from -3 to 0
- decay_rate: float32 [8, 128], P('pipe', ('dp', 'tensor')), may hold values from 0.005 to 0.5
- skip_gain: float32 [8, 128], P('pipe', ('dp', 'tensor')), may hold values from 0.5 to 1.5
- inner_gain: float32 [8, 8192], P('pipe', ('dp', 'tensor')), may hold values from 0.5 to 1.5
- w_out: bfloat16 [8, 8192, 4096], P('pipe', ('dp', 'tensor')), may hold values from -0.0625 to 0.0625
Outputs:
- activations: bfloat16 [8, 4, 64, 4096], P('pipe', None, ('dp', 'tensor'))
The draws below stay inside these ranges and needn't reach their ends.
Inputs may be any that keep to these rules, and one draw needn't show every extreme that they name: slice_order is a permutation of the slices.
All inputs are finite; a program needn't handle non-finite values.
Results may differ from the reference program's by a relative error of at most 0.029.
Values may be sent and summed in bfloat16 or wider, within the bound.
A program may use at most 64 MiB of HBM per device.

```python
import math
import jax
import jax.numpy as jnp
from jax import lax

D = 4096
HEADS = 128
HEAD_DIM = 64
STATE = 128
GROUPS = 8
CONV = 4
SLICE = 64
SLICES = 4
INNER = 8192
LAYERS = 8
N_PIPE = 8


def shard_levels(rng, extent, shards, least, high):
    gain = 1.0
    for axis_at, parts in shards:
        draws = jax.random.uniform(jax.random.fold_in(jax.random.fold_in(rng, 6), axis_at), (parts,), jnp.float32, least / len(shards), high / len(shards))
        gain = gain * jnp.repeat(jnp.exp(draws), extent[axis_at] // parts).reshape((-1,) + (1,) * (len(extent) - 1 - axis_at))
    return gain


def scatter_about(rng, dims, deviation, limit, shards=(), held_as=jnp.bfloat16):
    level = shard_levels(rng, dims, shards, -0.22, 0.18) if shards else 1.0
    values = jax.random.normal(rng, dims, jnp.float32) * deviation * level
    return jnp.minimum(jnp.maximum(values, -limit), limit).astype(held_as)


def setup_inputs(seed: int = 0) -> dict:
    arg_keys = jax.random.split(jax.random.key(seed), 15)
    tokens = scatter_about(arg_keys[0], (SLICES, SLICE, D), 1.0, 6.0)
    slice_order = jax.random.permutation(arg_keys[1], SLICES).astype(jnp.int32)
    norm_gain = jnp.clip(1.0 + 0.1 * jax.random.normal(arg_keys[2], (LAYERS, D), jnp.float32), 0.5, 1.5)
    w_z = scatter_about(arg_keys[3], (LAYERS, D, INNER), D ** -0.5, 0.09375, ((0, 8), (2, 16)))
    w_x = scatter_about(arg_keys[4], (LAYERS, D, INNER), D ** -0.5, 0.09375, ((0, 8), (2, 16)))
    w_bc = scatter_about(arg_keys[5], (LAYERS, D, GROUPS * 2 * STATE), D ** -0.5, 0.09375, ((0, 8), (2, 8)))
    w_dt = scatter_about(arg_keys[6], (LAYERS, D, HEADS), D ** -0.5, 0.09375, ((0, 8), (2, 16)))
    conv_x = scatter_about(arg_keys[7], (LAYERS, CONV, INNER), 0.5, 3.0, ((0, 8), (2, 16)), jnp.float32)
    conv_bc = scatter_about(arg_keys[8], (LAYERS, CONV, GROUPS * 2 * STATE), 0.5, 3.0, ((0, 8), (2, 8)), jnp.float32)
    dt_bias = jnp.clip(-3.0 + 3.0 * jax.random.uniform(arg_keys[9], (LAYERS, HEADS), jnp.float32) ** shard_levels(arg_keys[9], (LAYERS, HEADS), ((0, 8), (1, 16)), -0.2, 0.2), -3.0, 0.0)
    decay_rate = jnp.clip(jnp.exp(math.log(0.5) - 4.6051702 * jax.random.uniform(arg_keys[10], (LAYERS, HEADS), jnp.float32) ** shard_levels(arg_keys[10], (LAYERS, HEADS), ((0, 8), (1, 16)), -0.2, 0.2)), 0.005, 0.5)
    skip_gain = jnp.clip(0.5 + 1.0 * jax.random.uniform(arg_keys[11], (LAYERS, HEADS), jnp.float32) ** shard_levels(arg_keys[11], (LAYERS, HEADS), ((0, 8), (1, 16)), -0.2, 0.2), 0.5, 1.5)
    inner_gain = jnp.clip(1.0 + 0.1 * jax.random.normal(arg_keys[12], (LAYERS, INNER), jnp.float32), 0.5, 1.5)
    w_out = scatter_about(arg_keys[13], (LAYERS, INNER, D), INNER ** -0.5, 0.0625, ((0, 8), (1, 16)))
    return dict(tokens=tokens, slice_order=slice_order, norm_gain=norm_gain, w_z=w_z, w_x=w_x, w_bc=w_bc, w_dt=w_dt, conv_x=conv_x, conv_bc=conv_bc, dt_bias=dt_bias, decay_rate=decay_rate, skip_gain=skip_gain, inner_gain=inner_gain, w_out=w_out)


EPS = 1e-05
HIGH = lax.Precision.HIGHEST

def mixer_part(rows_in, conv_state, bc_state, ssm_state, norm_gain, w_z, w_x, w_bc, w_dt, conv_x, conv_bc, dt_bias, decay_rate, skip_gain, head_pick, group_pick):
    length = rows_in.shape[0]
    heads = w_dt.shape[1]
    head_dim = w_x.shape[1] // heads
    taps = conv_x.shape[0]
    values = rows_in.astype(jnp.float32)
    normed = (values * lax.rsqrt(lax.optimization_barrier(jnp.mean(values * values, axis=1, keepdims=True)) + EPS) * norm_gain).astype(jnp.bfloat16)
    gate_in = jnp.dot(normed, w_z, preferred_element_type=jnp.float32)
    x_raw = jnp.dot(normed, w_x, preferred_element_type=jnp.float32)
    bc_raw = jnp.dot(normed, w_bc, preferred_element_type=jnp.float32)
    dt_raw = jnp.dot(normed, w_dt, preferred_element_type=jnp.float32)
    x_full = jnp.concatenate([conv_state, x_raw], axis=0)
    bc_full = jnp.concatenate([bc_state, bc_raw], axis=0)
    x_conv = jnp.zeros_like(x_raw)
    bc_conv = jnp.zeros_like(bc_raw)
    for k in range(taps):
        x_conv = x_conv + conv_x[k] * x_full[k:k + length]
        bc_conv = bc_conv + conv_bc[k] * bc_full[k:k + length]
    x_act = jax.nn.silu(x_conv)
    bc_act = jax.nn.silu(bc_conv)
    groups_here = head_pick.shape[1]
    bc_groups = bc_act.reshape(length, groups_here, 2 * STATE)
    b_head = jnp.einsum('hg,tgn->thn', head_pick, bc_groups[:, :, :STATE], precision=HIGH)
    c_head = jnp.einsum('hg,tgn->thn', head_pick, bc_groups[:, :, STATE:], precision=HIGH)
    step_size = jax.nn.softplus(dt_raw + dt_bias)
    cumulated = jnp.cumsum(-step_size * decay_rate, axis=0)
    x_heads = x_act.reshape(length, heads, head_dim)
    scores = jnp.einsum('thn,shn->hts', c_head, b_head, precision=HIGH)
    differences = cumulated.T[:, :, None] - cumulated.T[:, None, :]
    below_diag = (jnp.arange(length)[:, None] >= jnp.arange(length)[None, :])[None, :, :]
    decays = jnp.where(below_diag, jnp.exp(jnp.where(below_diag, differences, 0.0)), 0.0)
    weighted = x_heads * step_size[:, :, None]
    outputs = jnp.einsum('hts,shp->thp', scores * decays, weighted, precision=HIGH)
    outputs = outputs + jnp.exp(cumulated)[:, :, None] * jnp.einsum('thn,hpn->thp', c_head, ssm_state, precision=HIGH)
    outputs = outputs + skip_gain[None, :, None] * x_heads
    remaining = jnp.exp(cumulated[-1][None, :] - cumulated) * step_size
    new_state = jnp.exp(cumulated[-1])[:, None, None] * ssm_state + jnp.einsum('sh,shp,shn->hpn', remaining, x_heads, b_head, precision=HIGH)
    gated = outputs.reshape(length, heads * head_dim) * jax.nn.silu(gate_in)
    squares = jnp.dot(gated * gated, group_pick, precision=HIGH)
    return (gated, squares, x_full[length:], bc_full[length:], new_state)

def reference(tokens, slice_order, norm_gain, w_z, w_x, w_bc, w_dt, conv_x, conv_bc, dt_bias, decay_rate, skip_gain, inner_gain, w_out):
    ordered = tokens[slice_order]
    head_pick = (jnp.arange(GROUPS)[None, :] == (jnp.arange(HEADS) // (HEADS // GROUPS))[:, None]).astype(jnp.float32)
    group_pick = jnp.repeat(head_pick, HEAD_DIM, axis=0)
    channels = INNER // GROUPS
    current = ordered
    layer_outputs = []
    for layer in range(N_PIPE):

        def one_slice(carry, rows_in):
            conv_state, bc_state, ssm_state = carry
            gated, squares, conv_state, bc_state, ssm_state = mixer_part(rows_in, conv_state, bc_state, ssm_state, norm_gain[layer], w_z[layer], w_x[layer], w_bc[layer], w_dt[layer], conv_x[layer], conv_bc[layer], dt_bias[layer], decay_rate[layer], skip_gain[layer], head_pick, group_pick)
            scale = lax.rsqrt(jnp.dot(squares, group_pick.T, precision=HIGH) / channels + EPS)
            mixed = (gated * scale * inner_gain[layer]).astype(jnp.bfloat16)
            summed = jnp.dot(mixed, w_out[layer], preferred_element_type=jnp.float32)
            updated = (rows_in.astype(jnp.float32) + summed).astype(jnp.bfloat16)
            return ((conv_state, bc_state, ssm_state), updated)
        initial = (jnp.zeros((CONV - 1, INNER), jnp.float32), jnp.zeros((CONV - 1, GROUPS * 2 * STATE), jnp.float32), jnp.zeros((HEADS, HEAD_DIM, STATE), jnp.float32))
        finals, current = lax.scan(one_slice, initial, current)
        layer_outputs.append(current)
    return jnp.stack(layer_outputs)
```

```python
import functools

import jax
import jax.numpy as jnp
from jax import lax
from jax.experimental import pallas as pl
from jax.experimental.pallas import tpu as pltpu
from jax.sharding import PartitionSpec as P

MESH = pl.DeviceIdType.MESH
F32 = jnp.float32
BF16 = jnp.bfloat16
EPS = 1e-05
HIGH = lax.Precision.HIGHEST

SECTIONS = 8
MEMBERS = 16
SLICES = 4
LENGTH = 64
WIDTH = 4096
STATE = 128
CONV = 4
HEADS = 8
HEAD_DIM = 64
INNER = HEADS * HEAD_DIM
CHANNELS = 1024
ROWS = 16
COLS = 1024
WIDE = COLS + 128


def split_lanes(sums):
    high = sums.astype(BF16).astype(F32)
    lanes = lax.broadcasted_iota(jnp.int32, (sums.shape[0], 128), 1)
    return jnp.where(lanes < 64, high, sums - high).astype(BF16)


def join_lanes(terms):
    return terms + pltpu.roll(terms, 64, 1)


def silu(v):
    return v / (1.0 + jnp.exp(-v))


def kernel(
    order,
    tokens,
    norm_gain,
    w_z,
    w_x,
    w_bc,
    w_dt,
    conv_x,
    conv_bc,
    dt_bias,
    decay_rate,
    skip_gain,
    inner_gain,
    w_out,
    out,
    tokens_v,
    gain_v,
    next_gain,
    wz,
    wx,
    wbc,
    wdt,
    wout,
    cx,
    cbc,
    bias_v,
    rate_v,
    skip_v,
    inner_v,
    lhs,
    hop,
    held,
    sums_out,
    sums_in,
    fresh,
    ready,
    rows_in,
    x_hist,
    bc_hist,
    state,
    small_sem,
    weight_sem,
    gain_sem,
    lhs_send,
    lhs_recv,
    hop_send,
    hop_recv,
    held_send,
    held_recv,
    sums_send,
    sums_recv,
    rows_send,
    rows_recv,
):
    section = lax.axis_index("pipe")
    dp = lax.axis_index("dp")
    tensor = lax.axis_index("tensor")
    me = dp * 2 + tensor
    rb = lax.div(me, 4)
    fb = lax.rem(me, 4)
    my_x = tensor * 2 + lax.div(dp, 4)
    my_y = lax.rem(dp, 4)
    even = lax.rem(section, 2) == 0
    first = section == 0
    last = section == SECTIONS - 1

    def at_member(sec, member):
        return {"pipe": sec, "dp": lax.div(member, 2), "tensor": lax.rem(member, 2)}

    def at_offset(sec, d):
        x = lax.rem(my_x + lax.div(d, 4), 4)
        y = lax.rem(my_y + lax.rem(d, 4), 4)
        return {"pipe": sec, "dp": lax.rem(x, 2) * 4 + y, "tensor": lax.div(x, 2)}

    def remote(src, dst, send, recv, device):
        return pltpu.make_async_remote_copy(
            src_ref=src, dst_ref=dst, send_sem=send, recv_sem=recv, device_id=device, device_id_type=MESH
        )

    def wait_bytes(ref, sem):
        pltpu.make_async_copy(ref, ref, sem).wait()

    my_rows = pl.ds(pl.multiple_of(rb * ROWS, ROWS), ROWS)
    my_cols = pl.ds(pl.multiple_of(fb * COLS, COLS), COLS)

    small = [
        (conv_x.at[0], cx),
        (conv_bc.at[0], cbc),
        (dt_bias, bias_v),
        (decay_rate, rate_v),
        (skip_gain, skip_v),
        (inner_gain, inner_v),
        (norm_gain, gain_v),
    ]
    small_copies = [pltpu.make_async_copy(a, b, small_sem.at[i]) for i, (a, b) in enumerate(small)]
    token_copy = pltpu.make_async_copy(tokens, tokens_v, small_sem.at[len(small)])
    weights = [(w_dt, wdt), (w_bc, wbc), (w_x, wx), (w_z, wz), (w_out, wout)]
    weight_copies = [pltpu.make_async_copy(a.at[0], b, weight_sem.at[i]) for i, (a, b) in enumerate(weights)]
    for copy in small_copies:
        copy.start()

    @pl.when(first)
    def _():
        token_copy.start()

    for copy in weight_copies:
        copy.start()

    barrier = pltpu.get_barrier_semaphore()

    def greet(sec):
        def one(d, carry):
            pl.semaphore_signal(barrier, inc=1, device_id=at_offset(sec, d), device_id_type=MESH)
            return carry

        return one

    lax.fori_loop(1, MEMBERS, greet(section), 0)

    @pl.when(jnp.logical_not(even))
    def _():
        lax.fori_loop(0, MEMBERS, greet(section - 1), 0)

    @pl.when(jnp.logical_and(even, section > 0))
    def _():
        pl.semaphore_signal(barrier, inc=1, device_id=at_member(section - 1, me), device_id_type=MESH)

    @pl.when(section < SECTIONS - 1)
    def _():
        pl.semaphore_signal(barrier, inc=1, device_id=at_member(section + 1, me), device_id_type=MESH)

    x_hist[0:8, :] = jnp.zeros((8, INNER), F32)
    bc_hist[0:8, :] = jnp.zeros((8, 2 * STATE), F32)
    state[...] = jnp.zeros((STATE, INNER), F32)

    to_next = jnp.where(even, MEMBERS, jnp.where(last, 0, 1))
    to_previous = jnp.where(first, 0, 1)
    pl.semaphore_wait(barrier, MEMBERS - 1 + to_next + to_previous)

    gain_copy = remote(norm_gain, next_gain, gain_sem.at[0], gain_sem.at[1], at_member(section - 1, me))

    @pl.when(section > 0)
    def _():
        gain_copy.start()

    for copy in small_copies:
        copy.wait()

    @pl.when(first)
    def _():
        token_copy.wait()

    for copy in weight_copies:
        copy.wait()

    @pl.when(section < SECTIONS - 1)
    def _():
        gain_copy.wait_recv()

    def step(k, carry):
        @pl.when(first)
        def _():
            place = order[k]
            for f in range(4):
                part = tokens_v[place, :, f * COLS : (f + 1) * COLS].astype(F32)
                lhs[k, f, :, 0:COLS] = (part * gain_v[0:1, f * COLS : (f + 1) * COLS]).astype(BF16)
                lhs[k, f, :, COLS:WIDE] = split_lanes(jnp.sum(part * part, axis=1, keepdims=True))
            held[k] = tokens_v[place, my_rows, my_cols]

        @pl.when(section > 0)
        def _():
            @pl.when(even)
            def _():
                wait_bytes(hop.at[k], hop_recv.at[k])

                def forward(d, carry):
                    remote(
                        hop.at[k], lhs.at[k, fb, my_rows], lhs_send.at[k], lhs_recv.at[k], at_offset(section, d)
                    ).start()
                    return carry

                lax.fori_loop(1, MEMBERS, forward, 0)
                pltpu.make_async_copy(hop.at[k], lhs.at[k, fb, my_rows], lhs_recv.at[k]).start()

            wait_bytes(lhs.at[k], lhs_recv.at[k])

        sums = lhs[k, 0, :, COLS:WIDE].astype(F32)
        for f in range(1, 4):
            sums = sums + lhs[k, f, :, COLS:WIDE].astype(F32)
        scale = lax.rsqrt(join_lanes(sums) * (1.0 / WIDTH) + EPS)

        def project(weight):
            total = jnp.dot(lhs[k, 0, :, 0:COLS], weight[0:COLS], preferred_element_type=F32)
            for f in range(1, 4):
                total = total + jnp.dot(
                    lhs[k, f, :, 0:COLS], weight[f * COLS : (f + 1) * COLS], preferred_element_type=F32
                )
            return total

        dt_raw = project(wdt) * scale[:, 0:HEADS]
        bc_hist[8:72, :] = project(wbc) * jnp.concatenate([scale] * 2, axis=1)
        x_hist[8:72, :] = project(wx) * jnp.concatenate([scale] * 4, axis=1)
        gate_in = project(wz) * jnp.concatenate([scale] * 4, axis=1)

        bc_conv = cbc[0:1, :] * bc_hist[5:69, :]
        x_conv = cx[0:1, :] * x_hist[5:69, :]
        for j in range(1, CONV):
            bc_conv = bc_conv + cbc[j : j + 1, :] * bc_hist[5 + j : 69 + j, :]
            x_conv = x_conv + cx[j : j + 1, :] * x_hist[5 + j : 69 + j, :]
        bc_act = silu(bc_conv)
        x_act = silu(x_conv)
        b_part = bc_act[:, 0:STATE].astype(BF16)
        c_part = bc_act[:, STATE:].astype(BF16)

        raised = dt_raw + bias_v[...]
        steps = jnp.maximum(raised, 0.0) + jnp.log1p(jnp.exp(-jnp.abs(raised)))
        t64 = lax.broadcasted_iota(jnp.int32, (LENGTH, LENGTH), 0)
        s64 = lax.broadcasted_iota(jnp.int32, (LENGTH, LENGTH), 1)
        lower = (t64 >= s64).astype(F32)
        cumulated = jnp.dot(lower, -steps * rate_v[...], precision=HIGH, preferred_element_type=F32)
        spread = (
            lax.div(lax.broadcasted_iota(jnp.int32, (HEADS, INNER), 1), HEAD_DIM)
            == lax.broadcasted_iota(jnp.int32, (HEADS, INNER), 0)
        ).astype(F32)
        cum_wide = jnp.dot(cumulated, spread, precision=HIGH, preferred_element_type=F32)
        step_wide = jnp.dot(steps, spread, precision=HIGH, preferred_element_type=F32)
        skip_wide = jnp.dot(skip_v[...], spread, precision=HIGH, preferred_element_type=F32)
        t_wide = lax.broadcasted_iota(jnp.int32, (LENGTH, INNER), 0)
        s_wide = lax.rem(lax.broadcasted_iota(jnp.int32, (LENGTH, INNER), 1), HEAD_DIM)
        on_diag = t_wide == s_wide
        cum_row = jnp.sum(jnp.where(on_diag, cum_wide, 0.0), axis=0, keepdims=True)
        step_row = jnp.sum(jnp.where(on_diag, step_wide, 0.0), axis=0, keepdims=True)
        decays = jnp.exp(jnp.where(t_wide >= s_wide, cum_wide - cum_row, -1e30)) * step_row

        scores = lax.dot_general(
            c_part,
            jnp.concatenate([b_part, b_part], axis=0),
            (((1,), (1,)), ((), ())),
            preferred_element_type=F32,
        )
        lanes = lax.broadcasted_iota(jnp.int32, (LENGTH, 128), 1)
        carried = jnp.dot(c_part, state[...].astype(BF16), preferred_element_type=F32)
        y = jnp.exp(cum_wide) * carried + skip_wide * x_act
        inside = []
        for j in range(4):
            cols = slice(128 * j, 128 * (j + 1))
            x_pair = x_act[:, cols]
            block = jnp.concatenate(
                [jnp.where(lanes < 64, x_pair, 0.0), jnp.where(lanes < 64, 0.0, x_pair)], axis=0
            ).astype(BF16)
            inside.append(jnp.dot((scores * decays[:, cols]).astype(BF16), block, preferred_element_type=F32))
        y = y + jnp.concatenate(inside, axis=1)

        gated = y * silu(gate_in)
        squares = split_lanes(jnp.sum(gated * gated, axis=1, keepdims=True))
        mixed = (gated * inner_v[...]).astype(BF16)

        for j in range(4):
            f = lax.rem(fb + 1 + j, 4)
            part = jnp.dot(
                mixed, wout[:, pl.ds(pl.multiple_of(f * COLS, COLS), COLS)], preferred_element_type=F32
            )
            sums_out[k, f, :, 0:COLS] = part.astype(BF16)
            sums_out[k, f, :, COLS:WIDE] = squares
            for i in range(4):
                r = lax.rem(rb + 1 + i, 4)
                block = sums_out.at[k, f, pl.ds(pl.multiple_of(r * ROWS, ROWS), ROWS)]
                if j == 3 and i == 3:
                    pltpu.make_async_copy(block, sums_in.at[k, me], sums_recv.at[k]).start()
                else:
                    remote(
                        block, sums_in.at[k, me], sums_send.at[k], sums_recv.at[k], at_member(section, r * 4 + f)
                    ).start()

        last_cum = cum_wide[LENGTH - 1 : LENGTH, :]
        remaining = x_act * (jnp.exp(last_cum - cum_wide) * step_wide)
        state[...] = jnp.exp(last_cum) * state[...] + lax.dot_general(
            b_part, remaining.astype(BF16), (((0,), (0,)), ((), ())), preferred_element_type=F32
        )
        x_hist[0:8, :] = x_hist[64:72, :]
        bc_hist[0:8, :] = bc_hist[64:72, :]

        @pl.when(section > 0)
        def _():
            wait_bytes(held.at[k], held_recv.at[k])

        wait_bytes(sums_in.at[k], sums_recv.at[k])
        total = held[k].astype(F32)
        for g in range(8):
            one, two = sums_in.at[k, 2 * g], sums_in.at[k, 2 * g + 1]
            sq = join_lanes(one[:, COLS:WIDE].astype(F32) + two[:, COLS:WIDE].astype(F32))
            factor = lax.rsqrt(sq * (1.0 / CHANNELS) + EPS)
            both = one[:, 0:COLS].astype(F32) + two[:, 0:COLS].astype(F32)
            total = total + both * jnp.concatenate([factor] * (COLS // 128), axis=1)
        updated = total.astype(BF16)
        fresh[k] = updated

        @pl.when(section < SECTIONS - 1)
        def _():
            value = updated.astype(F32)
            ready[k, :, 0:COLS] = (value * next_gain[0:1, my_cols]).astype(BF16)
            ready[k, :, COLS:WIDE] = split_lanes(jnp.sum(value * value, axis=1, keepdims=True))

            @pl.when(even)
            def _():
                def spread_out(d, carry):
                    remote(
                        ready.at[k],
                        lhs.at[k, fb, my_rows],
                        lhs_send.at[k],
                        lhs_recv.at[k],
                        at_offset(section + 1, d),
                    ).start()
                    return carry

                lax.fori_loop(0, MEMBERS, spread_out, 0)

            @pl.when(jnp.logical_not(even))
            def _():
                remote(
                    ready.at[k], hop.at[k], hop_send.at[k], hop_recv.at[k], at_member(section + 1, me)
                ).start()

            remote(
                fresh.at[k], held.at[k], held_send.at[k], held_recv.at[k], at_member(section + 1, me)
            ).start()

        for i in range(1, 4):
            remote(
                fresh.at[k],
                rows_in.at[k, fb],
                rows_send.at[k],
                rows_recv.at[k],
                at_member(section, rb * 4 + lax.rem(fb + i, 4)),
            ).start()
        pltpu.make_async_copy(fresh.at[k], rows_in.at[k, fb], rows_recv.at[k]).start()
        return carry

    lax.fori_loop(0, SLICES, step, 0)

    pick = (
        lax.broadcasted_iota(jnp.int32, (8, ROWS), 1) == lax.broadcasted_iota(jnp.int32, (8, ROWS), 0) + 4 * fb
    ).astype(BF16)
    for k in range(SLICES):
        wait_bytes(rows_in.at[k], rows_recv.at[k])
        for f in range(4):
            chosen = jnp.dot(pick, rows_in[k, f], preferred_element_type=F32)
            out[0, k, :, f * COLS : (f + 1) * COLS] = chosen[0:4].astype(BF16)

    def drain(k, carry):
        wait_bytes(sums_in.at[k, pl.ds(0, MEMBERS - 1)], sums_send.at[k])
        wait_bytes(rows_in.at[k, pl.ds(0, 3)], rows_send.at[k])

        @pl.when(section < SECTIONS - 1)
        def _():
            wait_bytes(held.at[k], held_send.at[k])

            @pl.when(jnp.logical_not(even))
            def _():
                wait_bytes(hop.at[k], hop_send.at[k])

        @pl.when(even)
        def _():
            wait_bytes(sums_in.at[k], lhs_send.at[k])

            @pl.when(section > 0)
            def _():
                wait_bytes(sums_in.at[k, pl.ds(0, MEMBERS - 1)], lhs_send.at[k])

        return carry

    lax.fori_loop(0, SLICES, drain, 0)

    @pl.when(section > 0)
    def _():
        gain_copy.wait_send()


def local(tokens, slice_order, *rest):
    hbm = pl.BlockSpec(memory_space=pltpu.HBM)
    dma = pltpu.SemaphoreType.DMA
    return pl.pallas_call(
        kernel,
        out_shape=jax.ShapeDtypeStruct((1, SLICES, LENGTH // MEMBERS, WIDTH), BF16),
        in_specs=[pl.BlockSpec(memory_space=pltpu.SMEM)] + [hbm] * (1 + len(rest)),
        out_specs=pl.BlockSpec(memory_space=pltpu.VMEM),
        scratch_shapes=[
            pltpu.VMEM((SLICES, LENGTH, WIDTH), BF16),
            pltpu.VMEM((1, WIDTH), F32),
            pltpu.VMEM((1, WIDTH), F32),
            pltpu.VMEM((WIDTH, INNER), BF16),
            pltpu.VMEM((WIDTH, INNER), BF16),
            pltpu.VMEM((WIDTH, 2 * STATE), BF16),
            pltpu.VMEM((WIDTH, HEADS), BF16),
            pltpu.VMEM((INNER, WIDTH), BF16),
            pltpu.VMEM((CONV, INNER), F32),
            pltpu.VMEM((CONV, 2 * STATE), F32),
            pltpu.VMEM((1, HEADS), F32),
            pltpu.VMEM((1, HEADS), F32),
            pltpu.VMEM((1, HEADS), F32),
            pltpu.VMEM((1, INNER), F32),
            pltpu.VMEM((SLICES, 4, LENGTH, WIDE), BF16),
            pltpu.VMEM((SLICES, ROWS, WIDE), BF16),
            pltpu.VMEM((SLICES, ROWS, COLS), BF16),
            pltpu.VMEM((SLICES, 4, LENGTH, WIDE), BF16),
            pltpu.VMEM((SLICES, MEMBERS, ROWS, WIDE), BF16),
            pltpu.VMEM((SLICES, ROWS, COLS), BF16),
            pltpu.VMEM((SLICES, ROWS, WIDE), BF16),
            pltpu.VMEM((SLICES, 4, ROWS, COLS), BF16),
            pltpu.VMEM((LENGTH + 8, INNER), F32),
            pltpu.VMEM((LENGTH + 8, 2 * STATE), F32),
            pltpu.VMEM((STATE, INNER), F32),
            dma((8,)),
            dma((5,)),
            dma((2,)),
            dma((SLICES,)),
            dma((SLICES,)),
            dma((SLICES,)),
            dma((SLICES,)),
            dma((SLICES,)),
            dma((SLICES,)),
            dma((SLICES,)),
            dma((SLICES,)),
            dma((SLICES,)),
            dma((SLICES,)),
        ],
        compiler_params=pltpu.CompilerParams(
            collective_id=0, has_side_effects=True, vmem_limit_bytes=48 * 1024 * 1024
        ),
    )(slice_order, tokens, *rest)


def solution(mesh):
    both = ("dp", "tensor")
    placed = (
        P(),
        P(),
        P("pipe", None),
        P("pipe", None, both),
        P("pipe", None, both),
        P("pipe", None, "dp"),
        P("pipe", None, both),
        P("pipe", None, both),
        P("pipe", None, "dp"),
        P("pipe", both),
        P("pipe", both),
        P("pipe", both),
        P("pipe", both),
        P("pipe", both, None),
    )
    return jax.shard_map(
        local,
        mesh=mesh,
        in_specs=placed,
        out_specs=P("pipe", None, both, None),
        check_vma=False,
    )
```

```python
import jax
import jax.numpy as jnp
from jax import lax
from jax.experimental import pallas as pl
from jax.experimental.pallas import tpu as pltpu
from jax.sharding import PartitionSpec as P

MESH = pl.DeviceIdType.MESH
F32 = jnp.float32
BF16 = jnp.bfloat16
EPS = 1e-05
HIGH = lax.Precision.HIGHEST

SECTIONS = 8
MEMBERS = 16
SLICES = 4
SLICE = 64
LENGTH = 32
PIECES = SLICES * SLICE // LENGTH
SKEW = 1
WIDTH = 4096
OWN = WIDTH // MEMBERS
STATE = 128
CONV = 4
HEADS = 8
HEAD_DIM = 64
INNER = HEADS * HEAD_DIM
CHANNELS = 1024
BD = 2 * STATE + 128
SENT = 2 * OWN + 128
GROUPS_IN = 2


def ring_distance(step):
    return min(step, 4 - step)


OFFSETS = sorted(
    [(dx, dy) for dx in range(4) for dy in range(4)],
    key=lambda o: -(ring_distance(o[0]) + ring_distance(o[1])),
)


def silu(v):
    return v / (1.0 + jnp.exp(-v))


def kernel(
    order,
    tokens,
    norm_gain,
    w_z,
    w_x,
    w_bc,
    w_dt,
    conv_x,
    conv_bc,
    dt_bias,
    decay_rate,
    skip_gain,
    inner_gain,
    w_out,
    out,
    tokens_v,
    gain_v,
    wz,
    wx,
    wbd,
    wdt,
    wout,
    cx,
    cbc,
    bias_v,
    rate_v,
    skip_v,
    inner_v,
    lhs,
    sums_out,
    sums_in,
    fresh,
    rows_out,
    x_hist,
    bc_hist,
    state,
    small_sem,
    weight_sem,
    out_sem,
    lhs_send,
    lhs_recv,
    sums_send,
    sums_recv,
    rows_send,
    rows_recv,
):
    section = lax.axis_index("pipe")
    dp = lax.axis_index("dp")
    tensor = lax.axis_index("tensor")
    me = dp * 2 + tensor
    my_x = tensor * 2 + lax.div(dp, 4)
    my_y = lax.rem(dp, 4)
    first = section == 0
    last = section == SECTIONS - 1

    def member(dx, dy):
        x, y = lax.rem(my_x + dx, 4), lax.rem(my_y + dy, 4)
        return (lax.rem(x, 2) * 4 + y) * 2 + lax.div(x, 2)

    def device(sec, m):
        return {"pipe": sec, "dp": lax.div(m, 2), "tensor": lax.rem(m, 2)}

    targets = [member(dx, dy) for dx, dy in OFFSETS]
    sources = [member(4 - dx, 4 - dy) for dx, dy in OFFSETS]

    def remote(src, dst, send, recv, sec, m):
        return pltpu.make_async_remote_copy(
            src_ref=src, dst_ref=dst, send_sem=send, recv_sem=recv, device_id=device(sec, m), device_id_type=MESH
        )

    def wait_bytes(ref, sem):
        pltpu.make_async_copy(ref, ref, sem).wait()

    small = [
        (norm_gain, gain_v),
        (w_dt.at[0], wdt),
        (conv_x.at[0], cx),
        (conv_bc.at[0], cbc),
        (dt_bias, bias_v),
        (decay_rate, rate_v),
        (skip_gain, skip_v),
        (inner_gain, inner_v),
    ]
    small_copies = [pltpu.make_async_copy(a, b, small_sem.at[i]) for i, (a, b) in enumerate(small)]
    token_copy = pltpu.make_async_copy(tokens, tokens_v, small_sem.at[len(small)])
    for copy in small_copies:
        copy.start()

    def weight_copies(c):
        rows = pl.ds(pl.multiple_of(c * OWN, OWN), OWN)
        return [
            pltpu.make_async_copy(w_bc.at[0, rows], wbd.at[rows, 0 : 2 * STATE], weight_sem.at[c, 0]),
            pltpu.make_async_copy(w_x.at[0, rows], wx.at[rows], weight_sem.at[c, 1]),
            pltpu.make_async_copy(w_z.at[0, rows], wz.at[rows], weight_sem.at[c, 2]),
        ]

    def out_copy(c):
        cols = pl.ds(pl.multiple_of(c * OWN, OWN), OWN)
        return pltpu.make_async_copy(w_out.at[0, :, cols], wout.at[c], out_sem.at[c])

    def load(c, carry):
        for copy in weight_copies(c):
            copy.start()
        return carry

    def load_out(c, carry):
        out_copy(c).start()
        return carry

    lax.fori_loop(0, MEMBERS, load, 0)

    @pl.when(first)
    def _():
        token_copy.start()

    lax.fori_loop(0, MEMBERS, load_out, 0)

    barrier = pltpu.get_barrier_semaphore()

    def greet(sec, members):
        for m in members:
            pl.semaphore_signal(barrier, inc=1, device_id=device(sec, m), device_id_type=MESH)

    greet(section, sources[:-1])

    @pl.when(section > 0)
    def _():
        greet(section - 1, sources)

    x_hist[0:8, :] = jnp.zeros((8, INNER), F32)
    bc_hist[0:8, :] = jnp.zeros((8, 2 * STATE), F32)
    state[...] = jnp.zeros((STATE, INNER), F32)
    for copy in small_copies:
        copy.wait()

    diagonal = lax.broadcasted_iota(jnp.int32, (OWN, OWN), 0) == lax.broadcasted_iota(jnp.int32, (OWN, OWN), 1)

    def fold(c, carry):
        rows = pl.ds(pl.multiple_of(c * OWN, OWN), OWN)
        along = gain_v[0:1, rows]
        down = jnp.sum(jnp.where(diagonal, along, 0.0), axis=1, keepdims=True)
        steps = jnp.concatenate([wdt[:, rows].astype(F32) * along, jnp.zeros((128 - HEADS, OWN), F32)], axis=0)
        wbd[rows, 2 * STATE : BD] = jnp.transpose(steps).astype(BF16)
        for copy in weight_copies(c):
            copy.wait()
        wbd[rows, 0 : 2 * STATE] = (wbd[rows, 0 : 2 * STATE].astype(F32) * down).astype(BF16)
        wx[rows, :] = (wx[rows, :].astype(F32) * down).astype(BF16)
        wz[rows, :] = (wz[rows, :].astype(F32) * down).astype(BF16)
        return carry

    lax.fori_loop(0, MEMBERS, fold, 0)

    @pl.when(first)
    def _():
        token_copy.wait()

    pl.semaphore_wait(barrier, MEMBERS - 1 + jnp.where(last, 0, MEMBERS))

    def load_out_wait(c, carry):
        out_copy(c).wait()
        return carry

    lax.fori_loop(0, MEMBERS, load_out_wait, 0)

    spread = (
        lax.div(lax.broadcasted_iota(jnp.int32, (HEADS, INNER), 1), HEAD_DIM)
        == lax.broadcasted_iota(jnp.int32, (HEADS, INNER), 0)
    ).astype(F32)
    spread_rows = (
        lax.div(lax.broadcasted_iota(jnp.int32, (HEADS, HEADS * LENGTH), 1), LENGTH)
        == lax.broadcasted_iota(jnp.int32, (HEADS, HEADS * LENGTH), 0)
    ).astype(F32)
    skip_wide = jnp.dot(skip_v[...], spread, precision=HIGH, preferred_element_type=F32)

    def front(k):
        @pl.when(first)
        def _():
            place = order[lax.div(k, 2)]
            rows = pl.ds(pl.multiple_of(lax.rem(k, 2) * LENGTH, LENGTH), LENGTH)
            for c in range(MEMBERS):
                lhs[k, c] = tokens_v[place, rows, c * OWN : (c + 1) * OWN]

        bd_sum = jnp.zeros((LENGTH, BD), F32)
        x_sum = jnp.zeros((LENGTH, INNER), F32)
        squares = jnp.zeros((LENGTH, OWN), F32)
        per_group = MEMBERS // GROUPS_IN
        for g in range(GROUPS_IN):

            @pl.when(section > 0)
            def _():
                wait_bytes(lhs.at[k, pl.ds(0, per_group)], lhs_recv.at[k, g])

            for i in range(g * per_group, (g + 1) * per_group):
                c = sources[i]
                rows = pl.ds(pl.multiple_of(c * OWN, OWN), OWN)
                block = lhs[k, c]
                bd_sum = bd_sum + jnp.dot(block, wbd[rows, :], preferred_element_type=F32)
                x_sum = x_sum + jnp.dot(block, wx[rows, :], preferred_element_type=F32)
                wide = block.astype(F32)
                squares = squares + wide * wide
        scale = lax.rsqrt(jnp.sum(squares, axis=1, keepdims=True) * (1.0 / WIDTH) + EPS)
        dt_raw = bd_sum[:, 2 * STATE : 2 * STATE + HEADS] * scale
        bc_hist[8 : LENGTH + 8, :] = bd_sum[:, 0 : 2 * STATE] * scale
        x_hist[8 : LENGTH + 8, :] = x_sum * scale

        bc_conv = cbc[0:1, :] * bc_hist[5 : LENGTH + 5, :]
        x_conv = cx[0:1, :] * x_hist[5 : LENGTH + 5, :]
        for j in range(1, CONV):
            bc_conv = bc_conv + cbc[j : j + 1, :] * bc_hist[5 + j : LENGTH + 5 + j, :]
            x_conv = x_conv + cx[j : j + 1, :] * x_hist[5 + j : LENGTH + 5 + j, :]
        bc_act = silu(bc_conv)
        x_act = silu(x_conv)
        b_part = bc_act[:, 0:STATE].astype(BF16)
        c_part = bc_act[:, STATE:].astype(BF16)

        raised = dt_raw + bias_v[...]
        steps = jnp.maximum(raised, 0.0) + jnp.log1p(jnp.exp(-jnp.abs(raised)))
        lower = (
            lax.broadcasted_iota(jnp.int32, (LENGTH, LENGTH), 0)
            >= lax.broadcasted_iota(jnp.int32, (LENGTH, LENGTH), 1)
        ).astype(F32)
        cumulated = jnp.dot(lower, -steps * rate_v[...], precision=HIGH, preferred_element_type=F32)
        ending = cumulated[LENGTH - 1 : LENGTH, :]
        cum_rows = jnp.dot(cumulated, spread_rows, precision=HIGH, preferred_element_type=F32)
        step_rows = jnp.dot(steps, spread_rows, precision=HIGH, preferred_element_type=F32)
        grown = jnp.dot(jnp.exp(cumulated), spread, precision=HIGH, preferred_element_type=F32)
        remains = jnp.dot(jnp.exp(ending - cumulated) * steps, spread, precision=HIGH, preferred_element_type=F32)
        t_wide = lax.broadcasted_iota(jnp.int32, (LENGTH, HEADS * LENGTH), 0)
        s_wide = lax.rem(lax.broadcasted_iota(jnp.int32, (LENGTH, HEADS * LENGTH), 1), LENGTH)
        on_diag = t_wide == s_wide
        cum_row = jnp.sum(jnp.where(on_diag, cum_rows, 0.0), axis=0, keepdims=True)
        step_row = jnp.sum(jnp.where(on_diag, step_rows, 0.0), axis=0, keepdims=True)
        decays = jnp.exp(jnp.where(t_wide >= s_wide, cum_rows - cum_row, -1e30)) * step_row

        scores = lax.dot_general(
            c_part, jnp.concatenate([b_part] * 4, axis=0), (((1,), (1,)), ((), ())), preferred_element_type=F32
        )
        weighted = (jnp.concatenate([scores] * 2, axis=1) * decays).astype(BF16)
        low = lax.broadcasted_iota(jnp.int32, (LENGTH, 128), 1) < HEAD_DIM
        blocks = []
        for h in range(HEADS):
            pair = x_act[:, 128 * (h // 2) : 128 * (h // 2 + 1)]
            mine = jnp.where(low, pair, 0.0) if h % 2 == 0 else jnp.where(low, 0.0, pair)
            parts = [mine if j == h // 2 else jnp.zeros((LENGTH, 128), F32) for j in range(HEADS // 2)]
            blocks.append(jnp.concatenate(parts, axis=1))
        inside = jnp.dot(weighted, jnp.concatenate(blocks, axis=0).astype(BF16), preferred_element_type=F32)
        carried = jnp.dot(c_part, state[...].astype(BF16), preferred_element_type=F32)
        y = inside + grown * carried + skip_wide * x_act

        z_sum = jnp.zeros((LENGTH, INNER), F32)
        for c in range(MEMBERS):
            z_sum = z_sum + jnp.dot(lhs[k, c], wz[c * OWN : (c + 1) * OWN, :], preferred_element_type=F32)
        gated = y * silu(z_sum * scale)
        mixed = (gated * inner_v[...]).astype(BF16)

        total = jnp.sum(gated * gated, axis=1, keepdims=True)
        high = total.astype(BF16).astype(F32)
        lane = lax.broadcasted_iota(jnp.int32, (16, 128), 1)
        even = lax.rem(lax.div(lane, 32), 2) == 0
        terms = jnp.where(
            lane < 64,
            jnp.where(even, high[0:16], high[16:32]),
            jnp.where(even, (total - high)[0:16], (total - high)[16:32]),
        ).astype(BF16)

        for i in range(MEMBERS):
            m = targets[i]
            part = jnp.dot(mixed, wout[m], preferred_element_type=F32).astype(BF16)
            sums_out[k, m, :, 0:OWN] = part[0:16]
            sums_out[k, m, :, OWN : 2 * OWN] = part[16:32]
            sums_out[k, m, :, 2 * OWN : SENT] = terms
            if i < MEMBERS - 1:
                remote(
                    sums_out.at[k, m], sums_in.at[k, me], sums_send.at[k], sums_recv.at[k], section, m
                ).start()
            else:
                pltpu.make_async_copy(sums_out.at[k, m], sums_in.at[k, me], sums_recv.at[k]).start()

        state[...] = grown[LENGTH - 1 : LENGTH, :] * state[...] + lax.dot_general(
            b_part, (x_act * remains).astype(BF16), (((0,), (0,)), ((), ())), preferred_element_type=F32
        )
        x_hist[0:8, :] = x_hist[LENGTH : LENGTH + 8, :]
        bc_hist[0:8, :] = bc_hist[LENGTH : LENGTH + 8, :]

    def back(k):
        wait_bytes(sums_in.at[k], sums_recv.at[k])
        lane = lax.broadcasted_iota(jnp.int32, (16, 128), 1)
        even = lax.rem(lax.div(lane, 32), 2) == 0
        held = lhs[k, me].astype(F32)
        upper, lower = held[0:16], held[16:32]
        for g in range(MEMBERS // 2):
            both = sums_in[k, 2 * g].astype(F32) + sums_in[k, 2 * g + 1].astype(F32)
            sq = both[:, 2 * OWN : SENT]
            sq = sq + pltpu.roll(sq, 64, 1)
            factor = lax.rsqrt(sq * (1.0 / CHANNELS) + EPS)
            other = pltpu.roll(factor, 32, 1)
            top, bottom = jnp.where(even, factor, other), jnp.where(even, other, factor)
            upper = upper + both[:, 0:OWN] * jnp.concatenate([top] * 2, axis=1)
            lower = lower + both[:, OWN : 2 * OWN] * jnp.concatenate([bottom] * 2, axis=1)
        fresh[k, 0:16, :] = upper.astype(BF16)
        fresh[k, 16:32, :] = lower.astype(BF16)

        @pl.when(section < SECTIONS - 1)
        def _():
            for i in range(MEMBERS):
                remote(
                    fresh.at[k],
                    lhs.at[k, me],
                    lhs_send.at[k],
                    lhs_recv.at[k, i // (MEMBERS // GROUPS_IN)],
                    section + 1,
                    targets[i],
                ).start()

    def step(i, carry):
        @pl.when(i < PIECES)
        def _():
            front(i)

        @pl.when(i >= SKEW)
        def _():
            back(i - SKEW)

        return carry

    lax.fori_loop(0, PIECES + SKEW, step, 0)

    for q in range(4):
        quad = jnp.concatenate(
            [fresh[2 * s + q // 2, 16 * (q % 2) : 16 * (q % 2) + 16, :] for s in range(SLICES)], axis=0
        )
        for i in range(4):
            to = lax.broadcasted_iota(jnp.int32, (16, 64), 0)
            of = lax.broadcasted_iota(jnp.int32, (16, 64), 1)
            pick = (of == lax.div(to, 4) * 16 + lax.rem(to, 4) + 4 * i).astype(BF16)
            rows_out[4 * q + i] = jnp.dot(pick, quad, preferred_element_type=F32).astype(BF16)
    mine = out.at[:, pl.ds(pl.multiple_of(me * OWN, OWN), OWN)]
    for i in range(MEMBERS):
        m = targets[i]
        if i < MEMBERS - 1:
            remote(rows_out.at[m], mine, rows_send.at[0], rows_recv.at[0], section, m).start()
        else:
            pltpu.make_async_copy(rows_out.at[m], mine, rows_recv.at[0]).start()

    def drain(k, carry):
        wait_bytes(sums_in.at[k, pl.ds(0, MEMBERS - 1)], sums_send.at[k])

        @pl.when(section < SECTIONS - 1)
        def _():
            wait_bytes(lhs.at[k], lhs_send.at[k])

        return carry

    lax.fori_loop(0, PIECES, drain, 0)
    wait_bytes(rows_out.at[pl.ds(0, MEMBERS - 1)], rows_send.at[0])
    wait_bytes(rows_out, rows_recv.at[0])


def local(tokens, slice_order, norm_gain, w_z, w_x, w_bc, w_dt, *rest):
    hbm = pl.BlockSpec(memory_space=pltpu.HBM)
    dma = pltpu.SemaphoreType.DMA
    args = (tokens, norm_gain, w_z, w_x, w_bc, jnp.swapaxes(w_dt, 1, 2), *rest)
    rows = pl.pallas_call(
        kernel,
        out_shape=jax.ShapeDtypeStruct((SLICES * SLICE // MEMBERS, WIDTH), BF16),
        in_specs=[pl.BlockSpec(memory_space=pltpu.SMEM)] + [hbm] * len(args),
        out_specs=pl.BlockSpec(memory_space=pltpu.VMEM),
        scratch_shapes=[
            pltpu.VMEM((SLICES, SLICE, WIDTH), BF16),
            pltpu.VMEM((1, WIDTH), F32),
            pltpu.VMEM((WIDTH, INNER), BF16),
            pltpu.VMEM((WIDTH, INNER), BF16),
            pltpu.VMEM((WIDTH, BD), BF16),
            pltpu.VMEM((HEADS, WIDTH), BF16),
            pltpu.VMEM((MEMBERS, INNER, OWN), BF16),
            pltpu.VMEM((CONV, INNER), F32),
            pltpu.VMEM((CONV, 2 * STATE), F32),
            pltpu.VMEM((1, HEADS), F32),
            pltpu.VMEM((1, HEADS), F32),
            pltpu.VMEM((1, HEADS), F32),
            pltpu.VMEM((1, INNER), F32),
            pltpu.VMEM((PIECES, MEMBERS, LENGTH, OWN), BF16),
            pltpu.VMEM((PIECES, MEMBERS, 16, SENT), BF16),
            pltpu.VMEM((PIECES, MEMBERS, 16, SENT), BF16),
            pltpu.VMEM((PIECES, LENGTH, OWN), BF16),
            pltpu.VMEM((MEMBERS, 16, OWN), BF16),
            pltpu.VMEM((LENGTH + 8, INNER), F32),
            pltpu.VMEM((LENGTH + 8, 2 * STATE), F32),
            pltpu.VMEM((STATE, INNER), F32),
            dma((9,)),
            dma((MEMBERS, 3)),
            dma((MEMBERS,)),
            dma((PIECES,)),
            dma((PIECES, GROUPS_IN)),
            dma((PIECES,)),
            dma((PIECES,)),
            dma((1,)),
            dma((1,)),
        ],
        compiler_params=pltpu.CompilerParams(
            collective_id=0, has_side_effects=True, vmem_limit_bytes=60 * 1024 * 1024
        ),
    )(slice_order, *args)
    return rows.reshape(1, SLICES, SLICE // MEMBERS, WIDTH)


def solution(mesh):
    both = ("dp", "tensor")
    placed = (
        P(),
        P(),
        P("pipe", None),
        P("pipe", None, both),
        P("pipe", None, both),
        P("pipe", None, "dp"),
        P("pipe", None, both),
        P("pipe", None, both),
        P("pipe", None, "dp"),
        P("pipe", both),
        P("pipe", both),
        P("pipe", both),
        P("pipe", both),
        P("pipe", both, None),
    )
    return jax.shard_map(
        local,
        mesh=mesh,
        in_specs=placed,
        out_specs=P("pipe", None, both, None),
        check_vma=False,
    )
```

```python
import jax
import jax.numpy as jnp
from jax import lax
from jax.experimental import pallas as pl
from jax.experimental.pallas import tpu as pltpu
from jax.sharding import PartitionSpec as P

MESH = pl.DeviceIdType.MESH
F32 = jnp.float32
BF16 = jnp.bfloat16
EPS = 1e-05

SECTIONS = 8
MEMBERS = 16
SLICES = 4
SLICE = 64
UNIT = 16
UNITS = SLICES * SLICE // UNIT
RUNS = ((2, 8),)
WIDTH = 4096
OWN = WIDTH // MEMBERS
STATE = 128
CONV = 4
HEADS = 8
HEAD_DIM = 64
INNER = HEADS * HEAD_DIM
CHANNELS = 1024
BD = 2 * STATE + 128
GROUPS_IN = 4


def ring_distance(step):
    return min(step, 4 - step)


OFFSETS = sorted(
    [(dx, dy) for dx in range(4) for dy in range(4)],
    key=lambda o: -(ring_distance(o[0]) + ring_distance(o[1])),
)


def terms_of(value, count):
    terms = []
    for _ in range(count):
        terms.append(value.astype(BF16).astype(F32))
        value = value - terms[-1]
    return terms


def spread_over(value, places, count):
    parts = [jnp.dot(t.astype(BF16), places, preferred_element_type=F32) for t in terms_of(value, count)]
    return sum(parts[1:], parts[0])


def silu(v):
    return v / (1.0 + jnp.exp(-v))


def kernel(
    order,
    tokens,
    norm_gain,
    w_z,
    w_x,
    w_bc,
    w_dt,
    conv_x,
    conv_bc,
    dt_bias,
    decay_rate,
    skip_gain,
    inner_gain,
    w_out,
    out,
    tokens_v,
    gain_v,
    wz,
    wx,
    wbd,
    wdt,
    wout,
    cx,
    cbc,
    bias_v,
    rate_v,
    skip_v,
    inner_v,
    lhs_refs,
    sums_out_refs,
    sums_in_refs,
    squares_out,
    squares_in,
    fresh,
    rows_out,
    x_hist,
    bc_hist,
    state,
    small_sem,
    weight_sem,
    out_sem,
    lhs_sends,
    lhs_recvs,
    sums_sends,
    sums_recvs,
    squares_send,
    squares_recv,
    rows_send,
    rows_recv,
):
    section = lax.axis_index("pipe")
    dp = lax.axis_index("dp")
    tensor = lax.axis_index("tensor")
    me = dp * 2 + tensor
    my_x = tensor * 2 + lax.div(dp, 4)
    my_y = lax.rem(dp, 4)
    first = section == 0
    last = section == SECTIONS - 1

    def member(dx, dy):
        x, y = lax.rem(my_x + dx, 4), lax.rem(my_y + dy, 4)
        return (lax.rem(x, 2) * 4 + y) * 2 + lax.div(x, 2)

    def device(sec, m):
        return {"pipe": sec, "dp": lax.div(m, 2), "tensor": lax.rem(m, 2)}

    targets = [member(dx, dy) for dx, dy in OFFSETS]
    sources = [member(4 - dx, 4 - dy) for dx, dy in OFFSETS]

    def remote(src, dst, send, recv, sec, m):
        return pltpu.make_async_remote_copy(
            src_ref=src, dst_ref=dst, send_sem=send, recv_sem=recv, device_id=device(sec, m), device_id_type=MESH
        )

    def wait_bytes(ref, sem):
        pltpu.make_async_copy(ref, ref, sem).wait()

    small = [
        (norm_gain, gain_v),
        (w_dt.at[0], wdt),
        (conv_x.at[0], cx),
        (conv_bc.at[0], cbc),
        (dt_bias, bias_v),
        (decay_rate, rate_v),
        (skip_gain, skip_v),
        (inner_gain, inner_v),
    ]
    small_copies = [pltpu.make_async_copy(a, b, small_sem.at[i]) for i, (a, b) in enumerate(small)]
    token_copy = pltpu.make_async_copy(tokens, tokens_v, small_sem.at[len(small)])
    for copy in small_copies:
        copy.start()

    def weight_copies(c):
        rows = pl.ds(pl.multiple_of(c * OWN, OWN), OWN)
        return [
            pltpu.make_async_copy(w_bc.at[0, rows], wbd.at[rows, 0 : 2 * STATE], weight_sem.at[c, 0]),
            pltpu.make_async_copy(w_x.at[0, rows], wx.at[rows], weight_sem.at[c, 1]),
            pltpu.make_async_copy(w_z.at[0, rows], wz.at[rows], weight_sem.at[c, 2]),
        ]

    def out_copy(c):
        cols = pl.ds(pl.multiple_of(c * OWN, OWN), OWN)
        return pltpu.make_async_copy(w_out.at[0, :, cols], wout.at[c], out_sem.at[c])

    def load(c, carry):
        for copy in weight_copies(c):
            copy.start()
        return carry

    def load_out(c, carry):
        out_copy(c).start()
        return carry

    @pl.when(first)
    def _():
        token_copy.start()

    lax.fori_loop(0, MEMBERS, load, 0)

    barrier = pltpu.get_barrier_semaphore()

    def greet(sec, members):
        for m in members:
            pl.semaphore_signal(barrier, inc=1, device_id=device(sec, m), device_id_type=MESH)

    greet(section, sources[:-1])

    @pl.when(section > 0)
    def _():
        greet(section - 1, sources)

    x_hist[0:8, :] = jnp.zeros((8, INNER), F32)
    bc_hist[0:8, :] = jnp.zeros((8, 2 * STATE), F32)
    state[...] = jnp.zeros((STATE, INNER), F32)
    for copy in small_copies:
        copy.wait()

    diagonal = lax.broadcasted_iota(jnp.int32, (OWN, OWN), 0) == lax.broadcasted_iota(jnp.int32, (OWN, OWN), 1)

    def fold(c, carry):
        rows = pl.ds(pl.multiple_of(c * OWN, OWN), OWN)
        along = gain_v[0:1, rows]
        down = jnp.sum(jnp.where(diagonal, along, 0.0), axis=1, keepdims=True)
        steps = jnp.concatenate([wdt[:, rows].astype(F32) * along, jnp.zeros((128 - HEADS, OWN), F32)], axis=0)
        wbd[rows, 2 * STATE : BD] = jnp.transpose(steps).astype(BF16)
        for copy in weight_copies(c):
            copy.wait()
        wbd[rows, 0 : 2 * STATE] = (wbd[rows, 0 : 2 * STATE].astype(F32) * down).astype(BF16)
        wx[rows, :] = (wx[rows, :].astype(F32) * down).astype(BF16)
        wz[rows, :] = (wz[rows, :].astype(F32) * down).astype(BF16)
        return carry

    lax.fori_loop(0, MEMBERS, fold, 0)
    lax.fori_loop(0, MEMBERS, load_out, 0)

    @pl.when(first)
    def _():
        token_copy.wait()

    pl.semaphore_wait(barrier, MEMBERS - 1 + jnp.where(last, 0, MEMBERS))

    def load_out_wait(c, carry):
        out_copy(c).wait()
        return carry

    spread = (
        lax.div(lax.broadcasted_iota(jnp.int32, (HEADS, INNER), 1), HEAD_DIM)
        == lax.broadcasted_iota(jnp.int32, (HEADS, INNER), 0)
    ).astype(BF16)
    skip_wide = spread_over(skip_v[...], spread, 3)

    def front(run, k, unit):
        units = RUNS[run][0]
        length = units * UNIT
        lhs, lhs_recv = lhs_refs[run], lhs_recvs[run]
        sums_out, sums_in = sums_out_refs[run], sums_in_refs[run]
        sums_send, sums_recv = sums_sends[run], sums_recvs[run]

        @pl.when(first)
        def _():
            for u in range(units):
                place = order[lax.div(unit + u, SLICE // UNIT)]
                rows = pl.ds(pl.multiple_of(lax.rem(unit + u, SLICE // UNIT) * UNIT, UNIT), UNIT)
                for c in range(MEMBERS):
                    lhs[k, c, u] = tokens_v[place, rows, c * OWN : (c + 1) * OWN]

        bd_sum = jnp.zeros((length, BD), F32)
        x_sum = jnp.zeros((length, INNER), F32)
        z_sum = jnp.zeros((length, INNER), F32)
        squares = jnp.zeros((length, OWN), F32)
        per_group = MEMBERS // GROUPS_IN
        for g in range(GROUPS_IN):

            @pl.when(section > 0)
            def _():
                wait_bytes(lhs.at[k, pl.ds(0, per_group)], lhs_recv.at[k, g])

            for i in range(g * per_group, (g + 1) * per_group):
                c = sources[i]
                rows = pl.ds(pl.multiple_of(c * OWN, OWN), OWN)
                block = lhs[k, c].reshape(length, OWN)
                bd_sum = bd_sum + jnp.dot(block, wbd[rows, :], preferred_element_type=F32)
                x_sum = x_sum + jnp.dot(block, wx[rows, :], preferred_element_type=F32)
                z_sum = z_sum + jnp.dot(block, wz[rows, :], preferred_element_type=F32)
                wide = block.astype(F32)
                squares = squares + wide * wide
        scale = lax.rsqrt(jnp.sum(squares, axis=1, keepdims=True) * (1.0 / WIDTH) + EPS)
        dt_raw = bd_sum[:, 2 * STATE : 2 * STATE + HEADS] * scale
        bc_hist[8 : length + 8, :] = bd_sum[:, 0 : 2 * STATE] * scale
        x_hist[8 : length + 8, :] = x_sum * scale

        bc_conv = cbc[0:1, :] * bc_hist[5 : length + 5, :]
        x_conv = cx[0:1, :] * x_hist[5 : length + 5, :]
        for j in range(1, CONV):
            bc_conv = bc_conv + cbc[j : j + 1, :] * bc_hist[5 + j : length + 5 + j, :]
            x_conv = x_conv + cx[j : j + 1, :] * x_hist[5 + j : length + 5 + j, :]
        bc_act = silu(bc_conv)
        x_act = silu(x_conv)
        b_part = bc_act[:, 0:STATE].astype(BF16)
        c_part = bc_act[:, STATE:].astype(BF16)

        spread_rows = (
            lax.div(lax.broadcasted_iota(jnp.int32, (HEADS, HEADS * length), 1), length)
            == lax.broadcasted_iota(jnp.int32, (HEADS, HEADS * length), 0)
        ).astype(BF16)
        raised = dt_raw + bias_v[...]
        steps = jnp.maximum(raised, 0.0) + jnp.log1p(jnp.exp(-jnp.abs(raised)))
        lower = (
            lax.broadcasted_iota(jnp.int32, (length, 3 * length), 0)
            >= lax.rem(lax.broadcasted_iota(jnp.int32, (length, 3 * length), 1), length)
        ).astype(BF16)
        falls = jnp.concatenate(terms_of(-steps * rate_v[...], 3), axis=0).astype(BF16)
        cumulated = jnp.dot(lower, falls, preferred_element_type=F32)
        ending = cumulated[length - 1 : length, :]
        cum_rows = spread_over(cumulated, spread_rows, 3)
        step_rows = spread_over(steps, spread_rows, 2)
        grown = spread_over(jnp.exp(cumulated), spread, 2)
        remains = spread_over(jnp.exp(ending - cumulated) * steps, spread, 2)
        t_wide = lax.broadcasted_iota(jnp.int32, (length, HEADS * length), 0)
        s_wide = lax.rem(lax.broadcasted_iota(jnp.int32, (length, HEADS * length), 1), length)
        on_diag = t_wide == s_wide
        cum_row = jnp.sum(jnp.where(on_diag, cum_rows, 0.0), axis=0, keepdims=True)
        step_row = jnp.sum(jnp.where(on_diag, step_rows, 0.0), axis=0, keepdims=True)
        decays = jnp.exp(jnp.where(t_wide >= s_wide, cum_rows - cum_row, -1e30)) * step_row

        scores = lax.dot_general(
            c_part, jnp.concatenate([b_part] * HEADS, axis=0), (((1,), (1,)), ((), ())), preferred_element_type=F32
        )
        weighted = (scores * decays).astype(BF16)
        low = lax.broadcasted_iota(jnp.int32, (length, 128), 1) < HEAD_DIM
        blocks = []
        for h in range(HEADS):
            pair = x_act[:, 128 * (h // 2) : 128 * (h // 2 + 1)]
            mine = jnp.where(low, pair, 0.0) if h % 2 == 0 else jnp.where(low, 0.0, pair)
            parts = [mine if j == h // 2 else jnp.zeros((length, 128), F32) for j in range(HEADS // 2)]
            blocks.append(jnp.concatenate(parts, axis=1))
        inside = jnp.dot(weighted, jnp.concatenate(blocks, axis=0).astype(BF16), preferred_element_type=F32)
        carried = jnp.dot(c_part, state[...].astype(BF16), preferred_element_type=F32)
        y = inside + grown * carried + skip_wide * x_act

        gated = y * silu(z_sum * scale)
        mixed = (gated * inner_v[...]).astype(BF16)

        total = jnp.sum(gated * gated, axis=1, keepdims=True)
        on_row = lax.broadcasted_iota(jnp.int32, (length, 128), 0) == lax.broadcasted_iota(
            jnp.int32, (length, 128), 1
        )
        squares_out[unit] = jnp.sum(jnp.where(on_row, total, 0.0), axis=0, keepdims=True)

        @pl.when(unit == 0)
        def _():
            lax.fori_loop(0, MEMBERS, load_out_wait, 0)

        for i in range(MEMBERS):
            there = squares_in.at[unit, me]
            if i < MEMBERS - 1:
                remote(
                    squares_out.at[unit], there, squares_send.at[unit], squares_recv.at[unit], section, targets[i]
                ).start()
            else:
                pltpu.make_async_copy(squares_out.at[unit], there, squares_recv.at[unit]).start()

        for i in range(MEMBERS):
            m = targets[i]
            part = jnp.dot(mixed, wout[m], preferred_element_type=F32).astype(BF16)
            sums_out[k, m] = part.reshape(units, UNIT, OWN)
            if i < MEMBERS - 1:
                remote(
                    sums_out.at[k, m], sums_in.at[k, me], sums_send.at[k], sums_recv.at[k], section, m
                ).start()
            else:
                pltpu.make_async_copy(sums_out.at[k, m], sums_in.at[k, me], sums_recv.at[k]).start()
        state[...] = grown[length - 1 : length, :] * state[...] + lax.dot_general(
            b_part, (x_act * remains).astype(BF16), (((0,), (0,)), ((), ())), preferred_element_type=F32
        )
        x_hist[0:8, :] = x_hist[length : length + 8, :]
        bc_hist[0:8, :] = bc_hist[length : length + 8, :]

    def back(run, k, unit):
        units, pieces = RUNS[run]
        lhs, sums_in = lhs_refs[run], sums_in_refs[run]
        length = units * UNIT
        wait_bytes(squares_in.at[unit], squares_recv.at[unit])
        on_row = lax.broadcasted_iota(jnp.int32, (length, 128), 0) == lax.broadcasted_iota(
            jnp.int32, (length, 128), 1
        )
        factors = []
        for g in range(MEMBERS // 2):
            total = squares_in[unit, 2 * g] + squares_in[unit, 2 * g + 1]
            along = lax.rsqrt(total * (1.0 / CHANNELS) + EPS)
            factors.append(jnp.sum(jnp.where(on_row, along, 0.0), axis=1, keepdims=True))
        wait_bytes(sums_in.at[k], sums_recvs[run].at[k])
        total = lhs[k, me].reshape(length, OWN).astype(F32)
        for g in range(MEMBERS // 2):
            both = sums_in[k, 2 * g].astype(F32) + sums_in[k, 2 * g + 1].astype(F32)
            total = total + both.reshape(length, OWN) * factors[g]
        updated = total.astype(BF16).reshape(units, UNIT, OWN)
        for u in range(units):
            fresh[unit + u] = updated[u]

        @pl.when(section < SECTIONS - 1)
        def _():
            for i in range(MEMBERS):
                remote(
                    fresh.at[pl.ds(unit, units)],
                    lhs.at[k, me],
                    lhs_sends[run].at[k],
                    lhs_recvs[run].at[k, i // (MEMBERS // GROUPS_IN)],
                    section + 1,
                    targets[i],
                ).start()

    def give_rows(quads):
        for q in quads:
            quad = jnp.concatenate([fresh[4 * s + q] for s in range(SLICES)], axis=0)
            for i in range(4):
                to = lax.broadcasted_iota(jnp.int32, (16, 64), 0)
                of = lax.broadcasted_iota(jnp.int32, (16, 64), 1)
                pick = (of == lax.div(to, 4) * 16 + lax.rem(to, 4) + 4 * i).astype(BF16)
                rows_out[4 * q + i] = jnp.dot(pick, quad, preferred_element_type=F32).astype(BF16)
        for q in quads:
            for i in range(4):
                m = 4 * q + i

                @pl.when(m != me)
                def _():
                    remote(rows_out.at[m], mine, rows_send.at[0], rows_recv.at[0], section, m).start()

                @pl.when(m == me)
                def _():
                    pltpu.make_async_copy(rows_out.at[m], mine, rows_recv.at[0]).start()

    mine = out.at[:, pl.ds(pl.multiple_of(me * OWN, OWN), OWN)]
    early = range(4 - RUNS[-1][0])

    base = 0
    for run, (units, pieces) in enumerate(RUNS):

        def step(k, carry, run=run, units=units, pieces=pieces, base=base):
            unit = base + k * units

            if run == len(RUNS) - 1 and early:

                @pl.when(k == pieces - 1)
                def _():
                    give_rows(early)

            front(run, k, unit)
            back(run, k, unit)
            return carry

        lax.fori_loop(0, pieces, step, 0)
        base += units * pieces

    give_rows(range(len(early), 4))

    base = 0
    for run, (units, pieces) in enumerate(RUNS):

        def drain(k, carry, run=run, units=units, base=base):
            unit = base + k * units
            wait_bytes(squares_in.at[unit, pl.ds(0, MEMBERS - 1)], squares_send.at[unit])
            wait_bytes(sums_in_refs[run].at[k, pl.ds(0, MEMBERS - 1)], sums_sends[run].at[k])

            @pl.when(section < SECTIONS - 1)
            def _():
                wait_bytes(lhs_refs[run].at[k], lhs_sends[run].at[k])

            return carry

        lax.fori_loop(0, pieces, drain, 0)
        base += units * pieces
    wait_bytes(rows_out.at[pl.ds(0, MEMBERS - 1)], rows_send.at[0])
    wait_bytes(rows_out, rows_recv.at[0])


def local(tokens, slice_order, norm_gain, w_z, w_x, w_bc, w_dt, *rest):
    hbm = pl.BlockSpec(memory_space=pltpu.HBM)
    dma = pltpu.SemaphoreType.DMA
    args = (tokens, norm_gain, w_z, w_x, w_bc, jnp.swapaxes(w_dt, 1, 2), *rest)
    rows = pl.pallas_call(
        kernel,
        out_shape=jax.ShapeDtypeStruct((SLICES * SLICE // MEMBERS, WIDTH), BF16),
        in_specs=[pl.BlockSpec(memory_space=pltpu.SMEM)] + [hbm] * len(args),
        out_specs=pl.BlockSpec(memory_space=pltpu.VMEM),
        scratch_shapes=[
            pltpu.VMEM((SLICES, SLICE, WIDTH), BF16),
            pltpu.VMEM((1, WIDTH), F32),
            pltpu.VMEM((WIDTH, INNER), BF16),
            pltpu.VMEM((WIDTH, INNER), BF16),
            pltpu.VMEM((WIDTH, BD), BF16),
            pltpu.VMEM((HEADS, WIDTH), BF16),
            pltpu.VMEM((MEMBERS, INNER, OWN), BF16),
            pltpu.VMEM((CONV, INNER), F32),
            pltpu.VMEM((CONV, 2 * STATE), F32),
            pltpu.VMEM((1, HEADS), F32),
            pltpu.VMEM((1, HEADS), F32),
            pltpu.VMEM((1, HEADS), F32),
            pltpu.VMEM((1, INNER), F32),
            [pltpu.VMEM((pieces, MEMBERS, units, UNIT, OWN), BF16) for units, pieces in RUNS],
            [pltpu.VMEM((pieces, MEMBERS, units, UNIT, OWN), BF16) for units, pieces in RUNS],
            [pltpu.VMEM((pieces, MEMBERS, units, UNIT, OWN), BF16) for units, pieces in RUNS],
            pltpu.VMEM((UNITS, 1, 128), F32),
            pltpu.VMEM((UNITS, MEMBERS, 1, 128), F32),
            pltpu.VMEM((UNITS, UNIT, OWN), BF16),
            pltpu.VMEM((MEMBERS, 16, OWN), BF16),
            pltpu.VMEM((SLICE + 8, INNER), F32),
            pltpu.VMEM((SLICE + 8, 2 * STATE), F32),
            pltpu.VMEM((STATE, INNER), F32),
            dma((9,)),
            dma((MEMBERS, 3)),
            dma((MEMBERS,)),
            [dma((pieces,)) for _, pieces in RUNS],
            [dma((pieces, GROUPS_IN)) for _, pieces in RUNS],
            [dma((pieces,)) for _, pieces in RUNS],
            [dma((pieces,)) for _, pieces in RUNS],
            dma((UNITS,)),
            dma((UNITS,)),
            dma((1,)),
            dma((1,)),
        ],
        compiler_params=pltpu.CompilerParams(
            collective_id=0, has_side_effects=True, vmem_limit_bytes=60 * 1024 * 1024
        ),
    )(slice_order, *args)
    return rows.reshape(1, SLICES, SLICE // MEMBERS, WIDTH)


def solution(mesh):
    both = ("dp", "tensor")
    placed = (
        P(),
        P(),
        P("pipe", None),
        P("pipe", None, both),
        P("pipe", None, both),
        P("pipe", None, "dp"),
        P("pipe", None, both),
        P("pipe", None, both),
        P("pipe", None, "dp"),
        P("pipe", both),
        P("pipe", both),
        P("pipe", both),
        P("pipe", both),
        P("pipe", both, None),
    )
    return jax.shard_map(
        local,
        mesh=mesh,
        in_specs=placed,
        out_specs=P("pipe", None, both, None),
        check_vma=False,
    )
```

```python
import jax
import jax.numpy as jnp
from jax import lax
from jax.experimental import pallas as pl
from jax.experimental.pallas import tpu as pltpu
from jax.sharding import PartitionSpec as P

MESH = pl.DeviceIdType.MESH
F32 = jnp.float32
BF16 = jnp.bfloat16
EPS = 1e-05

SECTIONS = 8
MEMBERS = 16
SLICES = 4
SLICE = 64
UNIT = 16
UNITS = SLICES * SLICE // UNIT
RUNS = ((2, 8),)
WIDTH = 4096
OWN = WIDTH // MEMBERS
STATE = 128
CONV = 4
HEADS = 8
HEAD_DIM = 64
INNER = HEADS * HEAD_DIM
CHANNELS = 1024
BD = 2 * STATE + 128
GROUPS_IN = 4


def ring_distance(step):
    return min(step, 4 - step)


OFFSETS = sorted(
    [(dx, dy) for dx in range(4) for dy in range(4)],
    key=lambda o: -(ring_distance(o[0]) + ring_distance(o[1])),
)


def terms_of(value, count):
    terms = []
    for _ in range(count):
        terms.append(value.astype(BF16).astype(F32))
        value = value - terms[-1]
    return terms


def spread_over(value, places, count):
    parts = [jnp.dot(t.astype(BF16), places, preferred_element_type=F32) for t in terms_of(value, count)]
    return sum(parts[1:], parts[0])


def silu(v):
    return v / (1.0 + jnp.exp(-v))


def kernel(
    order,
    tokens,
    norm_gain,
    w_z,
    w_x,
    w_bc,
    w_dt,
    conv_x,
    conv_bc,
    dt_bias,
    decay_rate,
    skip_gain,
    inner_gain,
    w_out,
    out,
    tokens_v,
    gain_v,
    wz,
    wx,
    wbd,
    wdt,
    wout,
    cx,
    cbc,
    bias_v,
    rate_v,
    skip_v,
    inner_v,
    lhs_refs,
    sums_out_refs,
    sums_in_refs,
    squares_out,
    squares_in,
    fresh,
    rows_out,
    x_hist,
    bc_hist,
    state,
    small_sem,
    weight_sem,
    out_sem,
    lhs_sends,
    lhs_recvs,
    sums_sends,
    sums_recvs,
    squares_send,
    squares_recv,
    rows_send,
    rows_recv,
):
    section = lax.axis_index("pipe")
    dp = lax.axis_index("dp")
    tensor = lax.axis_index("tensor")
    me = dp * 2 + tensor
    my_x = tensor * 2 + lax.div(dp, 4)
    my_y = lax.rem(dp, 4)
    first = section == 0
    last = section == SECTIONS - 1

    def member(dx, dy):
        x, y = lax.rem(my_x + dx, 4), lax.rem(my_y + dy, 4)
        return (lax.rem(x, 2) * 4 + y) * 2 + lax.div(x, 2)

    def device(sec, m):
        return {"pipe": sec, "dp": lax.div(m, 2), "tensor": lax.rem(m, 2)}

    targets = [member(dx, dy) for dx, dy in OFFSETS]
    sources = [member(4 - dx, 4 - dy) for dx, dy in OFFSETS]

    def remote(src, dst, send, recv, sec, m):
        return pltpu.make_async_remote_copy(
            src_ref=src, dst_ref=dst, send_sem=send, recv_sem=recv, device_id=device(sec, m), device_id_type=MESH
        )

    def wait_bytes(ref, sem):
        pltpu.make_async_copy(ref, ref, sem).wait()

    small = [
        (norm_gain, gain_v),
        (w_dt.at[0], wdt),
        (conv_x.at[0], cx),
        (conv_bc.at[0], cbc),
        (dt_bias, bias_v),
        (decay_rate, rate_v),
        (skip_gain, skip_v),
        (inner_gain, inner_v),
    ]
    small_copies = [pltpu.make_async_copy(a, b, small_sem.at[i]) for i, (a, b) in enumerate(small)]
    token_copy = pltpu.make_async_copy(tokens, tokens_v, small_sem.at[len(small)])
    for copy in small_copies:
        copy.start()

    def weight_copies(c):
        rows = pl.ds(pl.multiple_of(c * OWN, OWN), OWN)
        return [
            pltpu.make_async_copy(w_bc.at[0, rows], wbd.at[rows, 0 : 2 * STATE], weight_sem.at[c, 0]),
            pltpu.make_async_copy(w_x.at[0, rows], wx.at[rows], weight_sem.at[c, 1]),
            pltpu.make_async_copy(w_z.at[0, rows], wz.at[rows], weight_sem.at[c, 2]),
        ]

    def out_copy(c):
        cols = pl.ds(pl.multiple_of(c * OWN, OWN), OWN)
        return pltpu.make_async_copy(w_out.at[0, :, cols], wout.at[c], out_sem.at[c])

    def load(c, carry):
        for copy in weight_copies(c):
            copy.start()
        return carry

    def load_out(c, carry):
        out_copy(c).start()
        return carry

    @pl.when(first)
    def _():
        token_copy.start()

    lax.fori_loop(0, MEMBERS, load, 0)

    barrier = pltpu.get_barrier_semaphore()

    def greet(sec, members):
        for m in members:
            pl.semaphore_signal(barrier, inc=1, device_id=device(sec, m), device_id_type=MESH)

    greet(section, sources[:-1])

    @pl.when(section > 0)
    def _():
        greet(section - 1, sources)

    x_hist[0:8, :] = jnp.zeros((8, INNER), F32)
    bc_hist[0:8, :] = jnp.zeros((8, 2 * STATE), F32)
    state[...] = jnp.zeros((STATE, INNER), F32)
    for copy in small_copies:
        copy.wait()

    diagonal = lax.broadcasted_iota(jnp.int32, (OWN, OWN), 0) == lax.broadcasted_iota(jnp.int32, (OWN, OWN), 1)

    def fold(c, carry):
        rows = pl.ds(pl.multiple_of(c * OWN, OWN), OWN)
        along = gain_v[0:1, rows]
        down = jnp.sum(jnp.where(diagonal, along, 0.0), axis=1, keepdims=True)
        steps = jnp.concatenate([wdt[:, rows].astype(F32) * along, jnp.zeros((128 - UNIT, OWN), F32)], axis=0)
        wbd[rows, 2 * STATE : BD] = jnp.transpose(steps).astype(BF16)
        for copy in weight_copies(c):
            copy.wait()
        wbd[rows, 0 : 2 * STATE] = (wbd[rows, 0 : 2 * STATE].astype(F32) * down).astype(BF16)
        wx[rows, :] = (wx[rows, :].astype(F32) * down).astype(BF16)
        wz[rows, :] = (wz[rows, :].astype(F32) * down).astype(BF16)
        return carry

    lax.fori_loop(0, MEMBERS, fold, 0)
    lax.fori_loop(0, MEMBERS, load_out, 0)

    @pl.when(first)
    def _():
        token_copy.wait()

    pl.semaphore_wait(barrier, MEMBERS - 1 + jnp.where(last, 0, MEMBERS))

    def load_out_wait(c, carry):
        out_copy(c).wait()
        return carry

    spread = (
        lax.div(lax.broadcasted_iota(jnp.int32, (HEADS, INNER), 1), HEAD_DIM)
        == lax.broadcasted_iota(jnp.int32, (HEADS, INNER), 0)
    ).astype(BF16)
    skip_wide = spread_over(skip_v[...], spread, 3)

    def front(run, k, unit):
        units = RUNS[run][0]
        length = units * UNIT
        lhs, lhs_recv = lhs_refs[run], lhs_recvs[run]
        sums_out, sums_in = sums_out_refs[run], sums_in_refs[run]
        sums_send, sums_recv = sums_sends[run], sums_recvs[run]

        @pl.when(first)
        def _():
            for u in range(units):
                place = order[lax.div(unit + u, SLICE // UNIT)]
                rows = pl.ds(pl.multiple_of(lax.rem(unit + u, SLICE // UNIT) * UNIT, UNIT), UNIT)
                for c in range(MEMBERS):
                    lhs[k, c, u] = tokens_v[place, rows, c * OWN : (c + 1) * OWN]

        bd_sum = jnp.zeros((length, BD), F32)
        x_sum = jnp.zeros((length, INNER), F32)
        z_sum = jnp.zeros((length, INNER), F32)
        squares = jnp.zeros((length, OWN), F32)
        per_group = MEMBERS // GROUPS_IN
        for g in range(GROUPS_IN):

            @pl.when(section > 0)
            def _():
                wait_bytes(lhs.at[k, pl.ds(0, per_group)], lhs_recv.at[k, g])

            for i in range(g * per_group, (g + 1) * per_group):
                c = sources[i]
                rows = pl.ds(pl.multiple_of(c * OWN, OWN), OWN)
                block = lhs[k, c].reshape(length, OWN)
                bd_sum = bd_sum + jnp.dot(block, wbd[rows, :], preferred_element_type=F32)
                x_sum = x_sum + jnp.dot(block, wx[rows, :], preferred_element_type=F32)
                z_sum = z_sum + jnp.dot(block, wz[rows, :], preferred_element_type=F32)
                wide = block.astype(F32)
                squares = squares + wide * wide
        scale = lax.rsqrt(jnp.sum(squares, axis=1, keepdims=True) * (1.0 / WIDTH) + EPS)
        dt_raw = bd_sum[:, 2 * STATE : 2 * STATE + HEADS] * scale
        bc_hist[8 : length + 8, :] = bd_sum[:, 0 : 2 * STATE] * scale
        x_hist[8 : length + 8, :] = x_sum * scale

        bc_conv = cbc[0:1, :] * bc_hist[5 : length + 5, :]
        x_conv = cx[0:1, :] * x_hist[5 : length + 5, :]
        for j in range(1, CONV):
            bc_conv = bc_conv + cbc[j : j + 1, :] * bc_hist[5 + j : length + 5 + j, :]
            x_conv = x_conv + cx[j : j + 1, :] * x_hist[5 + j : length + 5 + j, :]
        bc_act = silu(bc_conv)
        x_act = silu(x_conv)
        b_part = bc_act[:, 0:STATE].astype(BF16)
        c_part = bc_act[:, STATE:].astype(BF16)

        spread_rows = (
            lax.div(lax.broadcasted_iota(jnp.int32, (HEADS, HEADS * length), 1), length)
            == lax.broadcasted_iota(jnp.int32, (HEADS, HEADS * length), 0)
        ).astype(BF16)
        raised = dt_raw + bias_v[...]
        steps = jnp.maximum(raised, 0.0) + jnp.log1p(jnp.exp(-jnp.abs(raised)))
        lower = (
            lax.broadcasted_iota(jnp.int32, (length, 3 * length), 0)
            >= lax.rem(lax.broadcasted_iota(jnp.int32, (length, 3 * length), 1), length)
        ).astype(BF16)
        falls = jnp.concatenate(terms_of(-steps * rate_v[...], 3), axis=0).astype(BF16)
        cumulated = jnp.dot(lower, falls, preferred_element_type=F32)
        ending = cumulated[length - 1 : length, :]
        cum_rows = spread_over(cumulated, spread_rows, 3)
        step_rows = spread_over(steps, spread_rows, 2)
        grown = spread_over(jnp.exp(cumulated), spread, 2)
        remains = spread_over(jnp.exp(ending - cumulated) * steps, spread, 2)
        t_wide = lax.broadcasted_iota(jnp.int32, (length, HEADS * length), 0)
        s_wide = lax.rem(lax.broadcasted_iota(jnp.int32, (length, HEADS * length), 1), length)
        on_diag = t_wide == s_wide
        cum_row = jnp.sum(jnp.where(on_diag, cum_rows, 0.0), axis=0, keepdims=True)
        step_row = jnp.sum(jnp.where(on_diag, step_rows, 0.0), axis=0, keepdims=True)
        decays = jnp.exp(jnp.where(t_wide >= s_wide, cum_rows - cum_row, -1e30)) * step_row

        scores = lax.dot_general(
            c_part, jnp.concatenate([b_part] * HEADS, axis=0), (((1,), (1,)), ((), ())), preferred_element_type=F32
        )
        weighted = (scores * decays).astype(BF16)
        low = lax.broadcasted_iota(jnp.int32, (length, 128), 1) < HEAD_DIM
        blocks = []
        for h in range(HEADS):
            pair = x_act[:, 128 * (h // 2) : 128 * (h // 2 + 1)]
            mine = jnp.where(low, pair, 0.0) if h % 2 == 0 else jnp.where(low, 0.0, pair)
            parts = [mine if j == h // 2 else jnp.zeros((length, 128), F32) for j in range(HEADS // 2)]
            blocks.append(jnp.concatenate(parts, axis=1))
        inside = jnp.dot(weighted, jnp.concatenate(blocks, axis=0).astype(BF16), preferred_element_type=F32)
        carried = jnp.dot(c_part, state[...].astype(BF16), preferred_element_type=F32)
        y = inside + grown * carried + skip_wide * x_act

        gated = y * silu(z_sum * scale)
        mixed = (gated * inner_v[...]).astype(BF16)

        total = jnp.sum(gated * gated, axis=1, keepdims=True)
        on_row = lax.broadcasted_iota(jnp.int32, (length, 128), 0) == lax.broadcasted_iota(
            jnp.int32, (length, 128), 1
        )
        squares_out[unit] = jnp.sum(jnp.where(on_row, total, 0.0), axis=0, keepdims=True)

        @pl.when(unit == 0)
        def _():
            lax.fori_loop(0, MEMBERS, load_out_wait, 0)

        for i in range(MEMBERS):
            there = squares_in.at[unit, me]
            if i < MEMBERS - 1:
                remote(
                    squares_out.at[unit], there, squares_send.at[unit], squares_recv.at[unit], section, targets[i]
                ).start()
            else:
                pltpu.make_async_copy(squares_out.at[unit], there, squares_recv.at[unit]).start()

        for i in range(MEMBERS):
            m = targets[i]
            part = jnp.dot(mixed, wout[m], preferred_element_type=F32).astype(BF16)
            sums_out[k, m] = part.reshape(units, UNIT, OWN)
            if i < MEMBERS - 1:
                remote(
                    sums_out.at[k, m], sums_in.at[k, me], sums_send.at[k], sums_recv.at[k], section, m
                ).start()
            else:
                pltpu.make_async_copy(sums_out.at[k, m], sums_in.at[k, me], sums_recv.at[k]).start()
        state[...] = grown[length - 1 : length, :] * state[...] + lax.dot_general(
            b_part, (x_act * remains).astype(BF16), (((0,), (0,)), ((), ())), preferred_element_type=F32
        )
        x_hist[0:8, :] = x_hist[length : length + 8, :]
        bc_hist[0:8, :] = bc_hist[length : length + 8, :]

    def back(run, k, unit):
        units, pieces = RUNS[run]
        lhs, sums_in = lhs_refs[run], sums_in_refs[run]
        length = units * UNIT
        wait_bytes(squares_in.at[unit], squares_recv.at[unit])
        on_row = lax.broadcasted_iota(jnp.int32, (length, 128), 0) == lax.broadcasted_iota(
            jnp.int32, (length, 128), 1
        )
        factors = []
        for g in range(MEMBERS // 2):
            total = squares_in[unit, 2 * g] + squares_in[unit, 2 * g + 1]
            along = lax.rsqrt(total * (1.0 / CHANNELS) + EPS)
            factors.append(jnp.sum(jnp.where(on_row, along, 0.0), axis=1, keepdims=True))
        wait_bytes(sums_in.at[k], sums_recvs[run].at[k])
        total = lhs[k, me].reshape(length, OWN).astype(F32)
        for g in range(MEMBERS // 2):
            both = sums_in[k, 2 * g].astype(F32) + sums_in[k, 2 * g + 1].astype(F32)
            total = total + both.reshape(length, OWN) * factors[g]
        updated = total.astype(BF16).reshape(units, UNIT, OWN)
        for u in range(units):
            fresh[unit + u] = updated[u]

        @pl.when(section < SECTIONS - 1)
        def _():
            for i in range(MEMBERS):
                remote(
                    fresh.at[pl.ds(unit, units)],
                    lhs.at[k, me],
                    lhs_sends[run].at[k],
                    lhs_recvs[run].at[k, i // (MEMBERS // GROUPS_IN)],
                    section + 1,
                    targets[i],
                ).start()

    def give_rows(quads):
        for q in quads:
            quad = jnp.concatenate([fresh[4 * s + q] for s in range(SLICES)], axis=0)
            for i in range(4):
                to = lax.broadcasted_iota(jnp.int32, (16, 64), 0)
                of = lax.broadcasted_iota(jnp.int32, (16, 64), 1)
                pick = (of == lax.div(to, 4) * 16 + lax.rem(to, 4) + 4 * i).astype(BF16)
                rows_out[4 * q + i] = jnp.dot(pick, quad, preferred_element_type=F32).astype(BF16)
        for q in quads:
            for i in range(4):
                m = 4 * q + i

                @pl.when(m != me)
                def _():
                    remote(rows_out.at[m], mine, rows_send.at[0], rows_recv.at[0], section, m).start()

                @pl.when(m == me)
                def _():
                    pltpu.make_async_copy(rows_out.at[m], mine, rows_recv.at[0]).start()

    mine = out.at[:, pl.ds(pl.multiple_of(me * OWN, OWN), OWN)]
    early = range(4 - RUNS[-1][0])

    base = 0
    for run, (units, pieces) in enumerate(RUNS):

        def step(k, carry, run=run, units=units, pieces=pieces, base=base):
            unit = base + k * units

            if run == len(RUNS) - 1 and early:

                @pl.when(k == pieces - 1)
                def _():
                    give_rows(early)

            front(run, k, unit)
            back(run, k, unit)
            return carry

        lax.fori_loop(0, pieces, step, 0)
        base += units * pieces

    give_rows(range(len(early), 4))

    base = 0
    for run, (units, pieces) in enumerate(RUNS):

        def drain(k, carry, run=run, units=units, base=base):
            unit = base + k * units
            wait_bytes(squares_in.at[unit, pl.ds(0, MEMBERS - 1)], squares_send.at[unit])
            wait_bytes(sums_in_refs[run].at[k, pl.ds(0, MEMBERS - 1)], sums_sends[run].at[k])

            @pl.when(section < SECTIONS - 1)
            def _():
                wait_bytes(lhs_refs[run].at[k], lhs_sends[run].at[k])

            return carry

        lax.fori_loop(0, pieces, drain, 0)
        base += units * pieces
    wait_bytes(rows_out.at[pl.ds(0, MEMBERS - 1)], rows_send.at[0])
    wait_bytes(rows_out, rows_recv.at[0])


def local(tokens, slice_order, norm_gain, w_z, w_x, w_bc, w_dt, *rest):
    hbm = pl.BlockSpec(memory_space=pltpu.HBM)
    dma = pltpu.SemaphoreType.DMA
    steps = jnp.pad(jnp.swapaxes(w_dt, 1, 2), ((0, 0), (0, UNIT - HEADS), (0, 0)))
    args = (tokens, norm_gain, w_z, w_x, w_bc, steps, *rest)
    rows = pl.pallas_call(
        kernel,
        out_shape=jax.ShapeDtypeStruct((SLICES * SLICE // MEMBERS, WIDTH), BF16),
        in_specs=[pl.BlockSpec(memory_space=pltpu.SMEM)] + [hbm] * len(args),
        out_specs=pl.BlockSpec(memory_space=pltpu.VMEM),
        scratch_shapes=[
            pltpu.VMEM((SLICES, SLICE, WIDTH), BF16),
            pltpu.VMEM((1, WIDTH), F32),
            pltpu.VMEM((WIDTH, INNER), BF16),
            pltpu.VMEM((WIDTH, INNER), BF16),
            pltpu.VMEM((WIDTH, BD), BF16),
            pltpu.VMEM((UNIT, WIDTH), BF16),
            pltpu.VMEM((MEMBERS, INNER, OWN), BF16),
            pltpu.VMEM((CONV, INNER), F32),
            pltpu.VMEM((CONV, 2 * STATE), F32),
            pltpu.VMEM((1, HEADS), F32),
            pltpu.VMEM((1, HEADS), F32),
            pltpu.VMEM((1, HEADS), F32),
            pltpu.VMEM((1, INNER), F32),
            [pltpu.VMEM((pieces, MEMBERS, units, UNIT, OWN), BF16) for units, pieces in RUNS],
            [pltpu.VMEM((pieces, MEMBERS, units, UNIT, OWN), BF16) for units, pieces in RUNS],
            [pltpu.VMEM((pieces, MEMBERS, units, UNIT, OWN), BF16) for units, pieces in RUNS],
            pltpu.VMEM((UNITS, 1, 128), F32),
            pltpu.VMEM((UNITS, MEMBERS, 1, 128), F32),
            pltpu.VMEM((UNITS, UNIT, OWN), BF16),
            pltpu.VMEM((MEMBERS, 16, OWN), BF16),
            pltpu.VMEM((SLICE + 8, INNER), F32),
            pltpu.VMEM((SLICE + 8, 2 * STATE), F32),
            pltpu.VMEM((STATE, INNER), F32),
            dma((9,)),
            dma((MEMBERS, 3)),
            dma((MEMBERS,)),
            [dma((pieces,)) for _, pieces in RUNS],
            [dma((pieces, GROUPS_IN)) for _, pieces in RUNS],
            [dma((pieces,)) for _, pieces in RUNS],
            [dma((pieces,)) for _, pieces in RUNS],
            dma((UNITS,)),
            dma((UNITS,)),
            dma((1,)),
            dma((1,)),
        ],
        compiler_params=pltpu.CompilerParams(
            collective_id=0, has_side_effects=True, vmem_limit_bytes=60 * 1024 * 1024
        ),
    )(slice_order, *args)
    return rows.reshape(1, SLICES, SLICE // MEMBERS, WIDTH)


def solution(mesh):
    both = ("dp", "tensor")
    placed = (
        P(),
        P(),
        P("pipe", None),
        P("pipe", None, both),
        P("pipe", None, both),
        P("pipe", None, "dp"),
        P("pipe", None, both),
        P("pipe", None, both),
        P("pipe", None, "dp"),
        P("pipe", both),
        P("pipe", both),
        P("pipe", both),
        P("pipe", both),
        P("pipe", both, None),
    )
    return jax.shard_map(
        local,
        mesh=mesh,
        in_specs=placed,
        out_specs=P("pipe", None, both, None),
        check_vma=False,
    )
```

```python
import jax
import jax.numpy as jnp
from jax import lax
from jax.experimental import pallas as pl
from jax.experimental.pallas import tpu as pltpu
from jax.sharding import PartitionSpec as P

MESH = pl.DeviceIdType.MESH
F32 = jnp.float32
BF16 = jnp.bfloat16
EPS = 1e-05

SECTIONS = 8
MEMBERS = 16
SLICES = 4
SLICE = 64
UNIT = 16
UNITS = SLICES * SLICE // UNIT
RUNS = ((2, 8),)
WIDTH = 4096
OWN = WIDTH // MEMBERS
STATE = 128
CONV = 4
HEADS = 8
HEAD_DIM = 64
INNER = HEADS * HEAD_DIM
CHANNELS = 1024
BD = 2 * STATE + 128
GROUPS_IN = 4


def ring_distance(step):
    return min(step, 4 - step)


OFFSETS = sorted(
    [(dx, dy) for dx in range(4) for dy in range(4)],
    key=lambda o: -(ring_distance(o[0]) + ring_distance(o[1])),
)


def terms_of(value, count):
    terms = []
    for _ in range(count):
        terms.append(value.astype(BF16).astype(F32))
        value = value - terms[-1]
    return terms


def spread_over(value, places, count):
    parts = [jnp.dot(t.astype(BF16), places, preferred_element_type=F32) for t in terms_of(value, count)]
    return sum(parts[1:], parts[0])


def silu(v):
    return v / (1.0 + jnp.exp(-v))


def kernel(
    order,
    tokens,
    norm_gain,
    w_z,
    w_x,
    w_bc,
    w_dt,
    conv_x,
    conv_bc,
    dt_bias,
    decay_rate,
    skip_gain,
    inner_gain,
    w_out,
    out,
    tokens_v,
    gain_v,
    wz,
    wx,
    wbd,
    wout,
    cx,
    cbc,
    bias_v,
    rate_v,
    skip_v,
    inner_v,
    lhs_refs,
    sums_out_refs,
    sums_in_refs,
    squares_out,
    squares_in,
    fresh,
    rows_out,
    x_hist,
    bc_hist,
    state,
    small_sem,
    weight_sem,
    out_sem,
    lhs_sends,
    lhs_recvs,
    sums_sends,
    sums_recvs,
    squares_send,
    squares_recv,
    rows_send,
    rows_recv,
):
    section = lax.axis_index("pipe")
    dp = lax.axis_index("dp")
    tensor = lax.axis_index("tensor")
    me = dp * 2 + tensor
    my_x = tensor * 2 + lax.div(dp, 4)
    my_y = lax.rem(dp, 4)
    first = section == 0
    last = section == SECTIONS - 1

    def member(dx, dy):
        x, y = lax.rem(my_x + dx, 4), lax.rem(my_y + dy, 4)
        return (lax.rem(x, 2) * 4 + y) * 2 + lax.div(x, 2)

    def device(sec, m):
        return {"pipe": sec, "dp": lax.div(m, 2), "tensor": lax.rem(m, 2)}

    targets = [member(dx, dy) for dx, dy in OFFSETS]
    sources = [member(4 - dx, 4 - dy) for dx, dy in OFFSETS]

    def remote(src, dst, send, recv, sec, m):
        return pltpu.make_async_remote_copy(
            src_ref=src, dst_ref=dst, send_sem=send, recv_sem=recv, device_id=device(sec, m), device_id_type=MESH
        )

    def wait_bytes(ref, sem):
        pltpu.make_async_copy(ref, ref, sem).wait()

    small = [
        (norm_gain, gain_v),
        (conv_x.at[0], cx),
        (conv_bc.at[0], cbc),
        (dt_bias, bias_v),
        (decay_rate, rate_v),
        (skip_gain, skip_v),
        (inner_gain, inner_v),
    ]
    small_copies = [pltpu.make_async_copy(a, b, small_sem.at[i]) for i, (a, b) in enumerate(small)]
    token_copy = pltpu.make_async_copy(tokens, tokens_v, small_sem.at[len(small)])
    for copy in small_copies:
        copy.start()

    def weight_copies(c):
        rows = pl.ds(pl.multiple_of(c * OWN, OWN), OWN)
        return [
            pltpu.make_async_copy(w_bc.at[0, rows], wbd.at[rows, 0 : 2 * STATE], weight_sem.at[c, 0]),
            pltpu.make_async_copy(w_x.at[0, rows], wx.at[rows], weight_sem.at[c, 1]),
            pltpu.make_async_copy(w_z.at[0, rows], wz.at[rows], weight_sem.at[c, 2]),
        ]

    def out_copy(c):
        cols = pl.ds(pl.multiple_of(c * OWN, OWN), OWN)
        return pltpu.make_async_copy(w_out.at[0, :, cols], wout.at[c], out_sem.at[c])

    def load(c, carry):
        for copy in weight_copies(c):
            copy.start()
        return carry

    def load_out(c, carry):
        out_copy(c).start()
        return carry

    @pl.when(first)
    def _():
        token_copy.start()

    lax.fori_loop(0, MEMBERS, load, 0)

    barrier = pltpu.get_barrier_semaphore()

    def greet(sec, members):
        for m in members:
            pl.semaphore_signal(barrier, inc=1, device_id=device(sec, m), device_id_type=MESH)

    greet(section, sources[:-1])

    @pl.when(section > 0)
    def _():
        greet(section - 1, sources)

    x_hist[0:8, :] = jnp.zeros((8, INNER), F32)
    bc_hist[0:8, :] = jnp.zeros((8, 2 * STATE), F32)
    state[...] = jnp.zeros((STATE, INNER), F32)
    for copy in small_copies:
        copy.wait()

    diagonal = lax.broadcasted_iota(jnp.int32, (OWN, OWN), 0) == lax.broadcasted_iota(jnp.int32, (OWN, OWN), 1)

    def fold(c, carry):
        rows = pl.ds(pl.multiple_of(c * OWN, OWN), OWN)
        along = gain_v[0:1, rows]
        down = jnp.sum(jnp.where(diagonal, along, 0.0), axis=1, keepdims=True)
        steps = jnp.concatenate([w_dt[0, :, rows].astype(F32) * along, jnp.zeros((128 - HEADS, OWN), F32)], axis=0)
        wbd[rows, 2 * STATE : BD] = jnp.transpose(steps).astype(BF16)
        for copy in weight_copies(c):
            copy.wait()
        wbd[rows, 0 : 2 * STATE] = (wbd[rows, 0 : 2 * STATE].astype(F32) * down).astype(BF16)
        wx[rows, :] = (wx[rows, :].astype(F32) * down).astype(BF16)
        wz[rows, :] = (wz[rows, :].astype(F32) * down).astype(BF16)
        return carry

    lax.fori_loop(0, MEMBERS, fold, 0)
    lax.fori_loop(0, MEMBERS, load_out, 0)

    @pl.when(first)
    def _():
        token_copy.wait()

    pl.semaphore_wait(barrier, MEMBERS - 1 + jnp.where(last, 0, MEMBERS))

    def load_out_wait(c, carry):
        out_copy(c).wait()
        return carry

    spread = (
        lax.div(lax.broadcasted_iota(jnp.int32, (HEADS, INNER), 1), HEAD_DIM)
        == lax.broadcasted_iota(jnp.int32, (HEADS, INNER), 0)
    ).astype(BF16)
    skip_wide = spread_over(skip_v[...], spread, 3)

    def front(run, k, unit):
        units = RUNS[run][0]
        length = units * UNIT
        lhs, lhs_recv = lhs_refs[run], lhs_recvs[run]
        sums_out, sums_in = sums_out_refs[run], sums_in_refs[run]
        sums_send, sums_recv = sums_sends[run], sums_recvs[run]

        @pl.when(first)
        def _():
            for u in range(units):
                place = order[lax.div(unit + u, SLICE // UNIT)]
                rows = pl.ds(pl.multiple_of(lax.rem(unit + u, SLICE // UNIT) * UNIT, UNIT), UNIT)
                for c in range(MEMBERS):
                    lhs[k, c, u] = tokens_v[place, rows, c * OWN : (c + 1) * OWN]

        bd_sum = jnp.zeros((length, BD), F32)
        x_sum = jnp.zeros((length, INNER), F32)
        z_sum = jnp.zeros((length, INNER), F32)
        squares = jnp.zeros((length, OWN), F32)
        per_group = MEMBERS // GROUPS_IN
        for g in range(GROUPS_IN):

            @pl.when(section > 0)
            def _():
                wait_bytes(lhs.at[k, pl.ds(0, per_group)], lhs_recv.at[k, g])

            for i in range(g * per_group, (g + 1) * per_group):
                c = sources[i]
                rows = pl.ds(pl.multiple_of(c * OWN, OWN), OWN)
                block = lhs[k, c].reshape(length, OWN)
                bd_sum = bd_sum + jnp.dot(block, wbd[rows, :], preferred_element_type=F32)
                x_sum = x_sum + jnp.dot(block, wx[rows, :], preferred_element_type=F32)
                z_sum = z_sum + jnp.dot(block, wz[rows, :], preferred_element_type=F32)
                wide = block.astype(F32)
                squares = squares + wide * wide
        scale = lax.rsqrt(jnp.sum(squares, axis=1, keepdims=True) * (1.0 / WIDTH) + EPS)
        dt_raw = bd_sum[:, 2 * STATE : 2 * STATE + HEADS] * scale
        bc_hist[8 : length + 8, :] = bd_sum[:, 0 : 2 * STATE] * scale
        x_hist[8 : length + 8, :] = x_sum * scale

        bc_conv = cbc[0:1, :] * bc_hist[5 : length + 5, :]
        x_conv = cx[0:1, :] * x_hist[5 : length + 5, :]
        for j in range(1, CONV):
            bc_conv = bc_conv + cbc[j : j + 1, :] * bc_hist[5 + j : length + 5 + j, :]
            x_conv = x_conv + cx[j : j + 1, :] * x_hist[5 + j : length + 5 + j, :]
        bc_act = silu(bc_conv)
        x_act = silu(x_conv)
        b_part = bc_act[:, 0:STATE].astype(BF16)
        c_part = bc_act[:, STATE:].astype(BF16)

        spread_rows = (
            lax.div(lax.broadcasted_iota(jnp.int32, (HEADS, HEADS * length), 1), length)
            == lax.broadcasted_iota(jnp.int32, (HEADS, HEADS * length), 0)
        ).astype(BF16)
        raised = dt_raw + bias_v[...]
        steps = jnp.maximum(raised, 0.0) + jnp.log1p(jnp.exp(-jnp.abs(raised)))
        lower = (
            lax.broadcasted_iota(jnp.int32, (length, 3 * length), 0)
            >= lax.rem(lax.broadcasted_iota(jnp.int32, (length, 3 * length), 1), length)
        ).astype(BF16)
        falls = jnp.concatenate(terms_of(-steps * rate_v[...], 3), axis=0).astype(BF16)
        cumulated = jnp.dot(lower, falls, preferred_element_type=F32)
        ending = cumulated[length - 1 : length, :]
        cum_rows = spread_over(cumulated, spread_rows, 3)
        step_rows = spread_over(steps, spread_rows, 2)
        grown = spread_over(jnp.exp(cumulated), spread, 2)
        remains = spread_over(jnp.exp(ending - cumulated) * steps, spread, 2)
        t_wide = lax.broadcasted_iota(jnp.int32, (length, HEADS * length), 0)
        s_wide = lax.rem(lax.broadcasted_iota(jnp.int32, (length, HEADS * length), 1), length)
        on_diag = t_wide == s_wide
        cum_row = jnp.sum(jnp.where(on_diag, cum_rows, 0.0), axis=0, keepdims=True)
        step_row = jnp.sum(jnp.where(on_diag, step_rows, 0.0), axis=0, keepdims=True)
        decays = jnp.exp(jnp.where(t_wide >= s_wide, cum_rows - cum_row, -1e30)) * step_row

        scores = lax.dot_general(
            c_part, jnp.concatenate([b_part] * HEADS, axis=0), (((1,), (1,)), ((), ())), preferred_element_type=F32
        )
        weighted = (scores * decays).astype(BF16)
        low = lax.broadcasted_iota(jnp.int32, (length, 128), 1) < HEAD_DIM
        blocks = []
        for h in range(HEADS):
            pair = x_act[:, 128 * (h // 2) : 128 * (h // 2 + 1)]
            mine = jnp.where(low, pair, 0.0) if h % 2 == 0 else jnp.where(low, 0.0, pair)
            parts = [mine if j == h // 2 else jnp.zeros((length, 128), F32) for j in range(HEADS // 2)]
            blocks.append(jnp.concatenate(parts, axis=1))
        inside = jnp.dot(weighted, jnp.concatenate(blocks, axis=0).astype(BF16), preferred_element_type=F32)
        carried = jnp.dot(c_part, state[...].astype(BF16), preferred_element_type=F32)
        y = inside + grown * carried + skip_wide * x_act

        gated = y * silu(z_sum * scale)
        mixed = (gated * inner_v[...]).astype(BF16)

        total = jnp.sum(gated * gated, axis=1, keepdims=True)
        on_row = lax.broadcasted_iota(jnp.int32, (length, 128), 0) == lax.broadcasted_iota(
            jnp.int32, (length, 128), 1
        )
        squares_out[unit] = jnp.sum(jnp.where(on_row, total, 0.0), axis=0, keepdims=True)

        @pl.when(unit == 0)
        def _():
            lax.fori_loop(0, MEMBERS, load_out_wait, 0)

        for i in range(MEMBERS):
            there = squares_in.at[unit, me]
            if i < MEMBERS - 1:
                remote(
                    squares_out.at[unit], there, squares_send.at[unit], squares_recv.at[unit], section, targets[i]
                ).start()
            else:
                pltpu.make_async_copy(squares_out.at[unit], there, squares_recv.at[unit]).start()

        for i in range(MEMBERS):
            m = targets[i]
            part = jnp.dot(mixed, wout[m], preferred_element_type=F32).astype(BF16)
            sums_out[k, m] = part.reshape(units, UNIT, OWN)
            if i < MEMBERS - 1:
                remote(
                    sums_out.at[k, m], sums_in.at[k, me], sums_send.at[k], sums_recv.at[k], section, m
                ).start()
            else:
                pltpu.make_async_copy(sums_out.at[k, m], sums_in.at[k, me], sums_recv.at[k]).start()
        state[...] = grown[length - 1 : length, :] * state[...] + lax.dot_general(
            b_part, (x_act * remains).astype(BF16), (((0,), (0,)), ((), ())), preferred_element_type=F32
        )
        x_hist[0:8, :] = x_hist[length : length + 8, :]
        bc_hist[0:8, :] = bc_hist[length : length + 8, :]

    def back(run, k, unit):
        units, pieces = RUNS[run]
        lhs, sums_in = lhs_refs[run], sums_in_refs[run]
        length = units * UNIT
        wait_bytes(squares_in.at[unit], squares_recv.at[unit])
        on_row = lax.broadcasted_iota(jnp.int32, (length, 128), 0) == lax.broadcasted_iota(
            jnp.int32, (length, 128), 1
        )
        factors = []
        for g in range(MEMBERS // 2):
            total = squares_in[unit, 2 * g] + squares_in[unit, 2 * g + 1]
            along = lax.rsqrt(total * (1.0 / CHANNELS) + EPS)
            factors.append(jnp.sum(jnp.where(on_row, along, 0.0), axis=1, keepdims=True))
        wait_bytes(sums_in.at[k], sums_recvs[run].at[k])
        total = lhs[k, me].reshape(length, OWN).astype(F32)
        for g in range(MEMBERS // 2):
            both = sums_in[k, 2 * g].astype(F32) + sums_in[k, 2 * g + 1].astype(F32)
            total = total + both.reshape(length, OWN) * factors[g]
        updated = total.astype(BF16).reshape(units, UNIT, OWN)
        for u in range(units):
            fresh[unit + u] = updated[u]

        @pl.when(section < SECTIONS - 1)
        def _():
            for i in range(MEMBERS):
                remote(
                    fresh.at[pl.ds(unit, units)],
                    lhs.at[k, me],
                    lhs_sends[run].at[k],
                    lhs_recvs[run].at[k, i // (MEMBERS // GROUPS_IN)],
                    section + 1,
                    targets[i],
                ).start()

    def give_rows(quads):
        for q in quads:
            quad = jnp.concatenate([fresh[4 * s + q] for s in range(SLICES)], axis=0)
            for i in range(4):
                to = lax.broadcasted_iota(jnp.int32, (16, 64), 0)
                of = lax.broadcasted_iota(jnp.int32, (16, 64), 1)
                pick = (of == lax.div(to, 4) * 16 + lax.rem(to, 4) + 4 * i).astype(BF16)
                rows_out[4 * q + i] = jnp.dot(pick, quad, preferred_element_type=F32).astype(BF16)
        for q in quads:
            for i in range(4):
                m = 4 * q + i

                @pl.when(m != me)
                def _():
                    remote(rows_out.at[m], mine, rows_send.at[0], rows_recv.at[0], section, m).start()

                @pl.when(m == me)
                def _():
                    pltpu.make_async_copy(rows_out.at[m], mine, rows_recv.at[0]).start()

    mine = out.at[:, pl.ds(pl.multiple_of(me * OWN, OWN), OWN)]
    early = range(4 - RUNS[-1][0])

    base = 0
    for run, (units, pieces) in enumerate(RUNS):

        def step(k, carry, run=run, units=units, pieces=pieces, base=base):
            unit = base + k * units

            if run == len(RUNS) - 1 and early:

                @pl.when(k == pieces - 1)
                def _():
                    give_rows(early)

            front(run, k, unit)
            back(run, k, unit)
            return carry

        lax.fori_loop(0, pieces, step, 0)
        base += units * pieces

    give_rows(range(len(early), 4))

    base = 0
    for run, (units, pieces) in enumerate(RUNS):

        def drain(k, carry, run=run, units=units, base=base):
            unit = base + k * units
            wait_bytes(squares_in.at[unit, pl.ds(0, MEMBERS - 1)], squares_send.at[unit])
            wait_bytes(sums_in_refs[run].at[k, pl.ds(0, MEMBERS - 1)], sums_sends[run].at[k])

            @pl.when(section < SECTIONS - 1)
            def _():
                wait_bytes(lhs_refs[run].at[k], lhs_sends[run].at[k])

            return carry

        lax.fori_loop(0, pieces, drain, 0)
        base += units * pieces
    wait_bytes(rows_out.at[pl.ds(0, MEMBERS - 1)], rows_send.at[0])
    wait_bytes(rows_out, rows_recv.at[0])


def local(tokens, slice_order, norm_gain, w_z, w_x, w_bc, w_dt, *rest):
    hbm = pl.BlockSpec(memory_space=pltpu.HBM)
    dma = pltpu.SemaphoreType.DMA
    args = (tokens, norm_gain, w_z, w_x, w_bc, jnp.swapaxes(w_dt, 1, 2), *rest)
    rows = pl.pallas_call(
        kernel,
        out_shape=jax.ShapeDtypeStruct((SLICES * SLICE // MEMBERS, WIDTH), BF16),
        in_specs=[pl.BlockSpec(memory_space=pltpu.SMEM)]
        + [pl.BlockSpec(memory_space=pltpu.VMEM) if i == 5 else hbm for i in range(len(args))],
        out_specs=pl.BlockSpec(memory_space=pltpu.VMEM),
        scratch_shapes=[
            pltpu.VMEM((SLICES, SLICE, WIDTH), BF16),
            pltpu.VMEM((1, WIDTH), F32),
            pltpu.VMEM((WIDTH, INNER), BF16),
            pltpu.VMEM((WIDTH, INNER), BF16),
            pltpu.VMEM((WIDTH, BD), BF16),
            pltpu.VMEM((MEMBERS, INNER, OWN), BF16),
            pltpu.VMEM((CONV, INNER), F32),
            pltpu.VMEM((CONV, 2 * STATE), F32),
            pltpu.VMEM((1, HEADS), F32),
            pltpu.VMEM((1, HEADS), F32),
            pltpu.VMEM((1, HEADS), F32),
            pltpu.VMEM((1, INNER), F32),
            [pltpu.VMEM((pieces, MEMBERS, units, UNIT, OWN), BF16) for units, pieces in RUNS],
            [pltpu.VMEM((pieces, MEMBERS, units, UNIT, OWN), BF16) for units, pieces in RUNS],
            [pltpu.VMEM((pieces, MEMBERS, units, UNIT, OWN), BF16) for units, pieces in RUNS],
            pltpu.VMEM((UNITS, 1, 128), F32),
            pltpu.VMEM((UNITS, MEMBERS, 1, 128), F32),
            pltpu.VMEM((UNITS, UNIT, OWN), BF16),
            pltpu.VMEM((MEMBERS, 16, OWN), BF16),
            pltpu.VMEM((SLICE + 8, INNER), F32),
            pltpu.VMEM((SLICE + 8, 2 * STATE), F32),
            pltpu.VMEM((STATE, INNER), F32),
            dma((9,)),
            dma((MEMBERS, 3)),
            dma((MEMBERS,)),
            [dma((pieces,)) for _, pieces in RUNS],
            [dma((pieces, GROUPS_IN)) for _, pieces in RUNS],
            [dma((pieces,)) for _, pieces in RUNS],
            [dma((pieces,)) for _, pieces in RUNS],
            dma((UNITS,)),
            dma((UNITS,)),
            dma((1,)),
            dma((1,)),
        ],
        compiler_params=pltpu.CompilerParams(
            collective_id=0, has_side_effects=True, vmem_limit_bytes=60 * 1024 * 1024
        ),
    )(slice_order, *args)
    return rows.reshape(1, SLICES, SLICE // MEMBERS, WIDTH)


def solution(mesh):
    both = ("dp", "tensor")
    placed = (
        P(),
        P(),
        P("pipe", None),
        P("pipe", None, both),
        P("pipe", None, both),
        P("pipe", None, "dp"),
        P("pipe", None, both),
        P("pipe", None, both),
        P("pipe", None, "dp"),
        P("pipe", both),
        P("pipe", both),
        P("pipe", both),
        P("pipe", both),
        P("pipe", both, None),
    )
    return jax.shard_map(
        local,
        mesh=mesh,
        in_specs=placed,
        out_specs=P("pipe", None, both, None),
        check_vma=False,
    )
```
